32 devices in a mesh: parts: 1, blk: 4 (over z), dp: 4 (over y, x), chan: 2 (over core).
Axes of the slice: x: 2, y: 2, z: 4, core: 2. Of those that a mesh axis runs over, the one named last changes fastest.
Arguments:
- fields: bfloat16 [4, 4, 1024, 1024], P('dp', 'parts', 'blk'), may hold values from -6 to 6
- lift_weight: bfloat16 [4, 32], P('parts'), may hold values from -3 to 3
- local_weight: bfloat16 [32, 32], P('parts', 'chan'), may hold values from -1 to 1
- spectral_weight: bfloat16 [2, 256, 32, 32, 256], P('parts', ('blk', 'dp'), 'chan'), may hold values from -3 to 3
- cotangent: bfloat16 [4, 32, 1024, 1024], P('dp', 'chan', 'blk', 'parts'), may hold values from -11 to 11
Outputs:
- spectral_grad: bfloat16 [2, 256, 32, 32, 256], P('parts', ('blk', 'dp'), 'chan')
- local_grad: float32 [32, 32], P('parts', 'chan')
- lift_grad: float32 [4, 32], P('parts')
The draws below stay inside these ranges and needn't reach their ends.
All inputs are finite; a program needn't handle non-finite values.
Results may differ from the reference program's by a relative error of at most 0.017.
Values may be sent and summed in bfloat16 or wider, within the bound.
No kernel may reach another device: no remote copies, remote signals or barrier semaphores. Data moves between devices by JAX's collectives and lax.ppermute only.
A program may use at most 320 MiB of HBM per device.

```python
import math
import jax
import jax.numpy as jnp
from jax import lax

NX = 1024
NY = 1024
C = 32
KR = 256
KC = 256
CIN = 4
BATCH = 4


def draw_cotangent(key, part):
    key = jax.random.fold_in(key, 11)
    full_shape = (BATCH, C, NX, NY)
    row_pos = jnp.arange(NX, dtype=jnp.float32) / NX
    sample_pos = jnp.arange(BATCH, dtype=jnp.float32) / max(BATCH - 1, 1)
    base_draw = jnp.clip(jax.random.normal(key, full_shape, jnp.float32), -4.0, 4.0)
    row_scale = 0.5 + row_pos
    sample_scale = 0.6 + 1.2 * sample_pos
    return (base_draw * row_scale[None, None, :, None] * sample_scale[:, None, None, None]).astype(jnp.bfloat16)


def levels(own_key, extent, cuts, smallest, top_value):
    level = 1.0
    for dim, blocks in cuts:
        heights = jax.random.uniform(jax.random.fold_in(jax.random.fold_in(own_key, 6), dim), (blocks,), jnp.float32, smallest / len(cuts), top_value / len(cuts))
        level = level * jnp.repeat(jnp.exp(heights), extent[dim] // blocks).reshape((-1,) + (1,) * (len(extent) - 1 - dim))
    return level


def noise(rng, extent, deviation, reach, pieces=(), held_as=jnp.bfloat16):
    drawn = jax.random.normal(rng, extent, jnp.float32) * deviation
    if len(pieces) > 0:
        drawn = levels(rng, extent, pieces, -0.22, 0.18) * drawn
    return jnp.clip(drawn, min=-reach, max=reach).astype(held_as)


def setup_inputs(seed: int = 0, part: int = 0) -> dict:
    arg_keys = jax.random.split(jax.random.key(seed), 6)
    part_splits = jax.random.split(jax.random.fold_in(arg_keys[5], part), 6)
    fields = noise(part_splits[0], (BATCH, CIN, NX, NY), 1.0, 6.0, ((0, 4), (2, 4)))
    lift_weight = noise(part_splits[1], (CIN, C), CIN ** -0.5, 3.0)
    local_weight = noise(part_splits[2], (C, C), C ** -0.5, 1.0, ((1, 2),))
    spectral_weight = noise(part_splits[3], (2, KR, C, C, KC), 0.5, 3.0, ((1, 16), (2, 2)))
    cotangent = draw_cotangent(jax.random.fold_in(jax.random.fold_in(arg_keys[5], part), 71), part)
    return dict(fields=fields, lift_weight=lift_weight, local_weight=local_weight, spectral_weight=spectral_weight, cotangent=cotangent)


TWO_PI = 2.0 * math.pi
HIGH = lax.Precision.HIGHEST

def phases(freqs, points, length):
    product = (freqs % length)[:, None] * points[None, :] % length
    return TWO_PI / length * product.astype(jnp.float32)

def row_freqs():
    index = jnp.arange(KR, dtype=jnp.int32)
    return jnp.where(index < KR // 2, index, index - KR)

def gelu_slope(value):
    return 0.5 * (1.0 + jax.scipy.special.erf(value / math.sqrt(2.0))) + value * jnp.exp(-0.5 * value * value) / math.sqrt(2.0 * math.pi)

def einsum_high(form, left, right):
    return jnp.einsum(form, left.astype(jnp.float32), right.astype(jnp.float32), precision=HIGH)

def make_tables():
    col_angle = phases(jnp.arange(KC, dtype=jnp.int32), jnp.arange(NY, dtype=jnp.int32), NY)
    row_angle = phases(row_freqs(), jnp.arange(NX, dtype=jnp.int32), NX)
    return (jnp.cos(col_angle).astype(jnp.bfloat16), (-jnp.sin(col_angle)).astype(jnp.bfloat16), jnp.cos(row_angle).astype(jnp.bfloat16), jnp.sin(row_angle).astype(jnp.bfloat16))

def to_spectrum(field, tables, scale):
    col_cos, col_sin, row_cos, row_sin = tables
    first_real = einsum_high('cry,ky->crk', field, col_cos).astype(jnp.bfloat16)
    first_imag = einsum_high('cry,ky->crk', field, col_sin).astype(jnp.bfloat16)
    real_part = einsum_high('mr,crk->cmk', row_cos, first_real) + einsum_high('mr,crk->cmk', row_sin, first_imag)
    imag_part = einsum_high('mr,crk->cmk', row_cos, first_imag) - einsum_high('mr,crk->cmk', row_sin, first_real)
    return ((real_part * scale).astype(jnp.bfloat16), (imag_part * scale).astype(jnp.bfloat16))

def to_grid(spec_real, spec_imag, tables, scale):
    col_cos, col_sin, row_cos, row_sin = tables
    half_real = (einsum_high('mr,cmk->crk', row_cos, spec_real) - einsum_high('mr,cmk->crk', row_sin, spec_imag)).astype(jnp.bfloat16)
    half_imag = (einsum_high('mr,cmk->crk', row_cos, spec_imag) + einsum_high('mr,cmk->crk', row_sin, spec_real)).astype(jnp.bfloat16)
    return scale * (einsum_high('crk,ky->cry', half_real, col_cos) + einsum_high('crk,ky->cry', half_imag, col_sin))

def reference(fields, lift_weight, local_weight, spectral_weight, cotangent):
    tables = make_tables()
    unit_scale = 1.0 / math.sqrt(NX * NY)
    norm_scale = 1.0 / math.sqrt(BATCH * NX * NY)

    def lifted_field(sample):
        lifted_pre = einsum_high('jry,jc->cry', sample, lift_weight)
        tanh_value = jnp.tanh(lifted_pre)
        return (tanh_value, tanh_value.astype(jnp.bfloat16))

    def forward_sample(sample):
        return to_spectrum(lifted_field(sample)[1], tables, unit_scale)
    field_real, field_imag = lax.map(forward_sample, fields)
    weight_real = spectral_weight[0]
    weight_imag = spectral_weight[1]
    out_real = (einsum_high('simk,miok->somk', field_real, weight_real) - einsum_high('simk,miok->somk', field_imag, weight_imag)).astype(jnp.bfloat16)
    out_imag = (einsum_high('simk,miok->somk', field_imag, weight_real) + einsum_high('simk,miok->somk', field_real, weight_imag)).astype(jnp.bfloat16)

    def middle_sample(items):
        sample, cotan, spec_real, spec_imag = items
        lifted = lifted_field(sample)[1]
        spatial = to_grid(spec_real, spec_imag, tables, 2.0 * unit_scale)
        pre_act = spatial + einsum_high('iry,io->ory', lifted, local_weight)
        grad_z = (cotan.astype(jnp.float32) * gelu_slope(pre_act)).astype(jnp.bfloat16)
        grad_real, grad_imag = to_spectrum(grad_z, tables, 2.0 * unit_scale)
        local_term = einsum_high('iry,ory->io', lifted, grad_z)
        return (grad_z, grad_real, grad_imag, local_term)
    grad_z, grad_real, grad_imag, local_terms = lax.map(middle_sample, (fields, cotangent, out_real, out_imag))
    local_grad = norm_scale * lax.optimization_barrier(jnp.sum(local_terms, axis=0))
    spec_grad_real = einsum_high('simk,somk->miok', field_real, grad_real) + einsum_high('simk,somk->miok', field_imag, grad_imag)
    spec_grad_imag = einsum_high('simk,somk->miok', field_real, grad_imag) - einsum_high('simk,somk->miok', field_imag, grad_real)
    spectral_grad = jnp.stack([spec_grad_real, spec_grad_imag], 0).astype(jnp.bfloat16)
    back_real = (einsum_high('somk,miok->simk', grad_real, weight_real) + einsum_high('somk,miok->simk', grad_imag, weight_imag)).astype(jnp.bfloat16)
    back_imag = (einsum_high('somk,miok->simk', grad_imag, weight_real) - einsum_high('somk,miok->simk', grad_real, weight_imag)).astype(jnp.bfloat16)

    def final_sample(items):
        sample, grad_sample, spec_real, spec_imag = items
        tanh_value = lifted_field(sample)[0]
        spatial = to_grid(spec_real, spec_imag, tables, unit_scale)
        grad_x = spatial + einsum_high('ory,io->iry', grad_sample, local_weight)
        grad_pre = grad_x * (1.0 - tanh_value * tanh_value)
        return einsum_high('jry,cry->jc', sample, grad_pre)
    lift_grad = norm_scale * lax.optimization_barrier(jnp.sum(lax.map(final_sample, (fields, grad_z, back_real, back_imag)), axis=0))
    return (spectral_grad, local_grad, lift_grad)
```

```python
import functools
import math

import jax
import jax.numpy as jnp
import ml_dtypes
import numpy as np
from jax import lax
from jax.experimental import pallas as pl
from jax.experimental.pallas import tpu as pltpu
from jax.sharding import PartitionSpec as P

BF = jnp.bfloat16
F32 = jnp.float32
TWO_PI = 2.0 * math.pi
CHUNKS = 1
VMEM = 48 * 1024 * 1024


def table(freqs, points, length):
    product = (freqs % length)[:, None] * points[None, :] % length
    angle = np.float32(TWO_PI / length) * product.astype(np.float32)
    return np.cos(angle), np.sin(angle)


def column_table(cells, modes):
    cos, sin = table(np.arange(modes), np.arange(cells), cells)
    width = modes // CHUNKS
    parts = []
    for c in range(CHUNKS):
        parts += [cos[c * width : (c + 1) * width], -sin[c * width : (c + 1) * width]]
    return np.ascontiguousarray(np.concatenate(parts, 0).T).astype(ml_dtypes.bfloat16)


def row_tables(rows, modes, blocks, samples):
    index = np.arange(modes)
    cos, sin = table(np.where(index < modes // 2, index, index - modes), np.arange(rows), rows)
    both = np.stack([cos, sin]).astype(ml_dtypes.bfloat16)
    sub = modes // (blocks * samples)
    local = rows // blocks
    out = np.empty((blocks, samples, 2 * modes, local), ml_dtypes.bfloat16)
    for z in range(blocks):
        part = both[:, :, z * local : (z + 1) * local]
        for s in range(samples):
            order = np.concatenate(
                [
                    np.arange(sub) + sub * ((s ^ j) + samples * ((z + d) % blocks))
                    for d in range(blocks)
                    for j in range(samples)
                ]
            )
            out[z, s] = part[:, order].reshape(2 * modes, local)
    return out


def gelu_slope(value):
    return 0.5 * (1.0 + lax.erf(value * (1.0 / math.sqrt(2.0)))) + value * jnp.exp(-0.5 * value * value) * (
        1.0 / math.sqrt(2.0 * math.pi)
    )


def row_forward(u, row_tab, scale, outs, at):
    modes = row_tab.shape[0] // 2
    blocks = len(outs[0])
    sub = modes // blocks
    for c, parts in enumerate(outs):
        width = u.shape[1] // (2 * len(outs))
        lo = 2 * width * c
        prod = jnp.dot(row_tab, u[:, lo : lo + 2 * width], preferred_element_type=F32)
        real = (prod[:modes, :width] + prod[modes:, width:]) * scale
        imag = (prod[:modes, width:] - prod[modes:, :width]) * scale
        for d, out in enumerate(parts):
            out[at, :, :width] = real[d * sub : (d + 1) * sub].astype(BF)
            out[at, :, width:] = imag[d * sub : (d + 1) * sub].astype(BF)


def row_inverse(parts, row_inv):
    rows = row_inv.shape[0] // 2
    halves = []
    for own, below, above in parts:
        width = own.shape[-1] // 2
        hops = len(below)
        blocks = [own[0]]
        for s in range(hops - 1, -1, -1):
            blocks.append(below[s][0] + above[hops - 1 - s][0])
        prod = jnp.dot(row_inv, jnp.concatenate(blocks, 0), preferred_element_type=F32)
        halves.append((prod[:rows, :width] - prod[rows:, width:]).astype(BF))
        halves.append((prod[:rows, width:] + prod[rows:, :width]).astype(BF))
    return jnp.concatenate(halves, 1)


def lift_kernel(blocks, scale, lw, fields, col, row_tab, lifted, *outs):
    group, rows, cells = lifted.shape
    inputs = fields.shape[0]
    first = pl.program_id(0) * group
    lanes = min(cells, 256)

    def lift_rows(step, _):
        at = pl.ds(pl.multiple_of(step * 16, 16), 16)
        for lo in range(0, cells, lanes):
            f = [fields[j, at, lo : lo + lanes].astype(F32) for j in range(inputs)]
            for c in range(group):
                total = f[0] * lw[0, first + c]
                for j in range(1, inputs):
                    total = total + f[j] * lw[j, first + c]
                lifted[c, at, lo : lo + lanes] = jnp.tanh(total).astype(BF)
        return 0

    lax.fori_loop(0, rows // 16, lift_rows, 0)
    outs = [outs[i : i + blocks] for i in range(0, len(outs), blocks)]
    for c in range(group):
        u = jnp.dot(lifted[c], col[...], preferred_element_type=F32).astype(BF)
        row_forward(u, row_tab[...], scale, outs, c)


def unpack_parts(refs, hops):
    each = 1 + 2 * hops
    return [
        (refs[i], refs[i + 1 : i + 1 + hops], refs[i + 1 + hops : i + each]) for i in range(0, len(refs), each)
    ]


def middle_kernel(blocks, parts, grid_scale, scale, local, cotan, col, col_inv, row_tab, row_inv, *refs):
    n_in = parts * (2 * blocks - 1)
    modes_in, grad, outs = unpack_parts(refs[:n_in], blocks - 1), refs[n_in], refs[n_in + 1 :]
    outs = [outs[i : i + blocks] for i in range(0, len(outs), blocks)]
    rows = grad.shape[1]
    h = row_inverse(modes_in, row_inv[...])
    step = min(rows, 64)
    pieces = []
    for lo in range(0, rows, step):
        grid = jnp.dot(h[lo : lo + step], col_inv[...], preferred_element_type=F32)
        pre = grid * grid_scale + local[0, lo : lo + step].astype(F32)
        g = (cotan[0, 0, lo : lo + step].astype(F32) * gelu_slope(pre)).astype(BF)
        grad[0, lo : lo + step] = g
        pieces.append(jnp.dot(g, col[...], preferred_element_type=F32).astype(BF))
    row_forward(jnp.concatenate(pieces, 0), row_tab[...], scale, outs, 0)


def final_kernel(blocks, parts, grid_scale, lw, fields, back_a, back_b, col_inv, row_inv, *refs):
    modes_in, out = unpack_parts(refs[:-1], blocks - 1), refs[-1]
    inputs, rows, cells = fields.shape
    chan = pl.program_id(0)
    h = row_inverse(modes_in, row_inv[...])
    step = min(rows, 32)
    sums = [jnp.zeros((8, 128), F32) for _ in range(inputs)]
    for lo in range(0, rows, step):
        grid = jnp.dot(h[lo : lo + step], col_inv[...], preferred_element_type=F32)
        total = (
            grid * grid_scale
            + back_a[0, lo : lo + step].astype(F32)
            + back_b[0, lo : lo + step].astype(F32)
        )
        f = [fields[j, lo : lo + step].astype(F32) for j in range(inputs)]
        pre = f[0] * lw[0, chan]
        for j in range(1, inputs):
            pre = pre + f[j] * lw[j, chan]
        t = jnp.tanh(pre)
        total = total * (1.0 - t * t)
        for j in range(inputs):
            prod = f[j] * total
            for a in range(0, step, 8):
                for b in range(0, cells, 128):
                    sums[j] = sums[j] + prod[a : a + 8, b : b + 128]
    for j in range(inputs):
        out[0, j] = sums[j]


def mix_kernel(samples, core, w_keep, w_send, *refs):
    xs, keep, send = refs[:samples], refs[samples], refs[samples + 1]
    width = w_keep.shape[-1]
    ins, outs = w_keep.shape[2], w_keep.shape[3]
    for lo in range(0, width, 128):
        re, im = pl.ds(lo, 128), pl.ds(width + lo, 128)
        xr = [x[0, :, re].astype(F32) for x in xs]
        xi = [x[0, :, im].astype(F32) for x in xs]
        for w, out in ((w_keep, keep), (w_send, send)):
            real = [jnp.zeros((outs, 128), F32) for _ in range(samples)]
            imag = [jnp.zeros((outs, 128), F32) for _ in range(samples)]
            for i in range(ins):
                wr = w[0, 0, i, :, re].astype(F32)
                wi = w[1, 0, i, :, re].astype(F32)
                for s in range(samples):
                    a, b = xr[s][i : i + 1], xi[s][i : i + 1]
                    real[s] = real[s] + (wr * a - wi * b)
                    imag[s] = imag[s] + (wr * b + wi * a)
            for s in range(samples):
                out[s, 0, :, re] = real[s].astype(BF)
                out[s, 0, :, im] = imag[s].astype(BF)


def back_kernel(samples, core, w_own, w_other, g_other, *refs):
    gs, out = refs[:samples], refs[samples]
    width = w_own.shape[-1]
    ins, outs = w_own.shape[2], w_own.shape[3]
    for lo in range(0, width, 128):
        re, im = pl.ds(lo, 128), pl.ds(width + lo, 128)
        gr = [[g[0, :, re].astype(F32) for g in gs], [g_other[s, 0, :, re].astype(F32) for s in range(samples)]]
        gi = [[g[0, :, im].astype(F32) for g in gs], [g_other[s, 0, :, im].astype(F32) for s in range(samples)]]
        real = [[] for _ in range(samples)]
        imag = [[] for _ in range(samples)]
        for i in range(ins):
            w = [
                (w_own[0, 0, i, :, re].astype(F32), w_own[1, 0, i, :, re].astype(F32)),
                (w_other[0, 0, i, :, re].astype(F32), w_other[1, 0, i, :, re].astype(F32)),
            ]
            for s in range(samples):
                r = m = None
                for half in range(2):
                    wr, wi = w[half]
                    a, b = gr[half][s], gi[half][s]
                    r1 = wr * a + wi * b
                    m1 = wr * b - wi * a
                    r, m = (r1, m1) if r is None else (r + r1, m + m1)
                real[s].append(jnp.sum(r, axis=0, keepdims=True))
                imag[s].append(jnp.sum(m, axis=0, keepdims=True))
        for s in range(samples):
            out[s, 0, :, re] = jnp.concatenate(real[s], 0).astype(BF)
            out[s, 0, :, im] = jnp.concatenate(imag[s], 0).astype(BF)


def weight_kernel(samples, parts, core, g_other, *refs):
    g_others = (g_other,) + refs[: parts - 1]
    refs = refs[parts - 1 :]
    out = refs[-1]
    xs = [refs[c * samples : (c + 1) * samples] for c in range(parts)]
    gs = [refs[(parts + c) * samples : (parts + c + 1) * samples] for c in range(parts)]
    ins, half = xs[0][0].shape[1], gs[0][0].shape[1]
    width = xs[0][0].shape[2] // 2
    own = pl.ds(pl.multiple_of(core[0] * half, half), half)
    other = pl.ds(pl.multiple_of((1 - core[0]) * half, half), half)
    for c in range(parts):
        for lo in range(0, width, 128):
            re, im, to = pl.ds(lo, 128), pl.ds(width + lo, 128), pl.ds(c * width + lo, 128)
            xr = [x[0, :, re].astype(F32) for x in xs[c]]
            xi = [x[0, :, im].astype(F32) for x in xs[c]]
            for where in (own, other):
                if where is own:
                    gr = [g[0, :, re].astype(F32) for g in gs[c]]
                    gi = [g[0, :, im].astype(F32) for g in gs[c]]
                else:
                    gr = [g_others[c][s, 0, :, re].astype(F32) for s in range(samples)]
                    gi = [g_others[c][s, 0, :, im].astype(F32) for s in range(samples)]
                for i in range(ins):
                    real = imag = None
                    for s in range(samples):
                        a, b = xr[s][i : i + 1], xi[s][i : i + 1]
                        r1 = gr[s] * a + gi[s] * b
                        m1 = gi[s] * a - gr[s] * b
                        real, imag = (r1, m1) if real is None else (real + r1, imag + m1)
                    out[0, 0, i, where, to] = real.astype(BF)
                    out[1, 0, i, where, to] = imag.astype(BF)


def call(body, grid, ins, outs, flops, transcendentals=0, prefetch=None):
    scalars = 0 if prefetch is None else 1

    def spec(block, index):
        if block is None:
            return pl.BlockSpec(memory_space=pltpu.SMEM)
        return pl.BlockSpec(block, index)

    moved = sum(a.size * a.dtype.itemsize for a, _, _ in ins) + sum(
        math.prod(s) * jnp.dtype(t).itemsize for s, t, _, _ in outs
    )
    got = pl.pallas_call(
        body,
        grid_spec=pltpu.PrefetchScalarGridSpec(
            num_scalar_prefetch=scalars,
            grid=grid,
            in_specs=[spec(b, i) for _, b, i in ins],
            out_specs=[spec(b, i) for _, _, b, i in outs],
        ),
        out_shape=[jax.ShapeDtypeStruct(s, t) for s, t, _, _ in outs],
        compiler_params=pltpu.CompilerParams(vmem_limit_bytes=VMEM),
        cost_estimate=pl.CostEstimate(flops=int(flops), bytes_accessed=int(moved), transcendentals=int(transcendentals)),
    )(*(() if prefetch is None else (prefetch,)), *[a for a, _, _ in ins])
    return got


def after(value, *earlier):
    return lax.optimization_barrier((value, *earlier))[0]


def chain_sum(parts):
    hops = len(parts) - 1
    blocks = hops + 1
    below = above = None
    for t in range(hops):
        up, down = parts[hops - t], parts[t + 1]
        if t:
            up = (up.astype(F32) + below.astype(F32)).astype(BF)
            down = (down.astype(F32) + above.astype(F32)).astype(BF)
        below = lax.ppermute(up, "blk", [(z, z + 1) for z in range(t + 1)])
        above = lax.ppermute(down, "blk", [(blocks - 1 - z, blocks - 2 - z) for z in range(t + 1)])
    return parts[0], below, above


def chain_gather(own, blocks):
    below, above = [], []
    up = down = own
    for t in range(blocks - 1):
        up = lax.ppermute(up, "blk", [(z, z + 1) for z in range(t, blocks - 1)])
        down = lax.ppermute(down, "blk", [(blocks - 1 - z, blocks - 2 - z) for z in range(t, blocks - 1)])
        below.append(up)
        above.append(down)
    return below, above


def swap_samples(pieces):
    n = len(pieces)
    return [pieces[0]] + [lax.ppermute(pieces[j], "dp", [(i, i ^ j) for i in range(n)]) for j in range(1, n)]


def swap_cores(value):
    return lax.ppermute(value, "chan", [(0, 1), (1, 0)])


def to_modes(parts, samples):
    own, below, above = chain_sum(parts)
    total = (own.astype(F32) + below.astype(F32) + above.astype(F32)).astype(BF)
    total = total.transpose(1, 0, 2)
    sub = total.shape[0] // samples
    return swap_samples([total[j * sub : (j + 1) * sub] for j in range(samples)])


def from_modes(pieces, blocks):
    own = jnp.concatenate(swap_samples(pieces), 0).transpose(1, 0, 2)
    below, above = chain_gather(own, blocks)
    return [own, *below, *above]


def all_sum(value, axes):
    for axis in axes:
        n = lax.axis_size(axis)
        step = 1
        while step < n:
            value = value + lax.ppermute(value, axis, [(i, i ^ step) for i in range(n)])
            step *= 2
    return value


def per_device(fields, lift_weight, local_weight, spectral_weight, cotangent):
    blocks = lax.axis_size("blk")
    samples = lax.axis_size("dp")
    sample = fields[0]
    inputs, rows, cells = sample.shape
    chans = cotangent.shape[1]
    mode_dev = spectral_weight.shape[1]
    half = spectral_weight.shape[3] // 2
    freqs = spectral_weight.shape[4]
    width = freqs // CHUNKS
    modes = mode_dev * blocks * samples
    sub = modes // blocks
    all_rows = rows * blocks
    z, s, core = lax.axis_index("blk"), lax.axis_index("dp"), lax.axis_index("chan")
    core_ref = core.astype(jnp.int32)[None]
    unit_scale = 1.0 / math.sqrt(all_rows * cells)
    norm_scale = 1.0 / math.sqrt(samples * all_rows * cells)

    col = jnp.asarray(column_table(cells, freqs))
    col_inv = jnp.asarray(np.ascontiguousarray(column_table(cells, freqs).T))
    row_tab = lax.dynamic_slice(
        jnp.asarray(row_tables(all_rows, modes, blocks, samples)), (z, s, 0, 0), (1, 1, 2 * modes, rows)
    )[0, 0]
    row_inv = row_tab.reshape(2, modes, rows).transpose(0, 2, 1).reshape(2 * rows, modes)
    own_lw = lax.dynamic_slice_in_dim(lift_weight.astype(F32), core * chans, chans, 1)

    def whole(a):
        return (a, a.shape, lambda i, *_: (0,) * a.ndim)

    def channel(a, n=1):
        return (a, (n, *a.shape[1:]), lambda i, *_: (i,) + (0,) * (a.ndim - 1))

    def part_outs(n):
        return [
            ((chans, sub, 2 * width), BF, (n, sub, 2 * width), lambda i, *_: (i, 0, 0))
            for _ in range(CHUNKS * blocks)
        ]

    matrix = chans * rows * 4 * freqs * (cells + 2 * modes)
    group = 2 if chans % 2 == 0 else 1
    lifted, *shares = call(
        functools.partial(lift_kernel, blocks, unit_scale),
        (chans // group,),
        [(own_lw, None, None), whole(sample), whole(col), whole(row_tab)],
        [(((chans, rows, cells)), BF, (group, rows, cells), lambda i, *_: (i, 0, 0)), *part_outs(group)],
        matrix,
        chans * rows * cells,
    )
    lifted_other = swap_cores(lifted)

    def weight_half(part, other):
        return (
            spectral_weight,
            (2, 1, chans, half, width),
            lambda i, c, part=part, other=other: (0, i, 0, (1 - c[0]) if other else c[0], part),
        )

    def row_mode(a):
        return (a, (1, *a.shape[1:]), lambda i, *_: (i, 0, 0))

    def stacked(a):
        return (a, (samples, 1, *a.shape[2:]), lambda i, *_: (0, i, 0, 0))

    mix_flops = 8 * samples * mode_dev * chans * 2 * half * width
    field_modes, out_parts = [], []
    for part in range(CHUNKS):
        mine = shares[part * blocks : (part + 1) * blocks]
        if part:
            mine = list(lax.optimization_barrier((*mine, *field_modes[-1]))[:blocks])
        xs = to_modes(mine, samples)
        field_modes.append(xs)
        shape = (samples, mode_dev, half, 2 * width)
        keep, send = call(
            functools.partial(mix_kernel, samples),
            (mode_dev,),
            [weight_half(part, False), weight_half(part, True), *[row_mode(x) for x in xs]],
            [(shape, BF, (samples, 1, half, 2 * width), lambda i, *_: (0, i, 0, 0))] * 2,
            mix_flops,
            prefetch=core_ref,
        )
        total = (keep.astype(F32) + swap_cores(send).astype(F32)).astype(BF)
        out_parts += from_modes([total[j] for j in range(samples)], blocks)

    own_rows = lax.dynamic_slice_in_dim(local_weight, core * chans, chans, 0)
    other_rows = lax.dynamic_slice_in_dim(local_weight, (1 - core) * chans, chans, 0)
    local = jnp.einsum("iry,io->ory", lifted, own_rows, preferred_element_type=F32) + jnp.einsum(
        "iry,io->ory", lifted_other, other_rows, preferred_element_type=F32
    )

    grad_z, *shares = call(
        functools.partial(middle_kernel, blocks, CHUNKS, 2.0 * unit_scale, 2.0 * unit_scale),
        (chans,),
        [
            channel(local),
            (cotangent, (1, 1, rows, cells), lambda i, *_: (0, i, 0, 0)),
            whole(col),
            whole(col_inv),
            whole(row_tab),
            whole(row_inv),
            *[channel(a) for a in out_parts],
        ],
        [((chans, rows, cells), BF, (1, rows, cells), lambda i, *_: (i, 0, 0)), *part_outs(1)],
        2 * matrix,
        3 * chans * rows * cells,
    )

    back_a = jnp.einsum("ory,io->iry", grad_z, own_rows, preferred_element_type=F32).astype(BF)
    back_b = swap_cores(
        jnp.einsum("ory,io->iry", grad_z, other_rows, preferred_element_type=F32).astype(BF)
    )
    term_own = jnp.einsum("iry,ory->io", lifted, grad_z, preferred_element_type=F32)
    term_other = jnp.einsum("iry,ory->io", lifted_other, grad_z, preferred_element_type=F32)
    terms = jnp.zeros(local_weight.shape, F32)
    terms = lax.dynamic_update_slice_in_dim(terms, term_own, core * chans, 0)
    terms = lax.dynamic_update_slice_in_dim(terms, term_other, (1 - core) * chans, 0)
    local_grad = all_sum(terms * norm_scale, ("dp", "blk"))

    grad_modes, grad_others, back_parts = [], [], []
    for part in range(CHUNKS):
        mine = shares[part * blocks : (part + 1) * blocks]
        if part:
            mine = list(lax.optimization_barrier((*mine, *grad_modes[-1]))[:blocks])
        gs = to_modes(mine, samples)
        grad_modes.append(gs)
        other = swap_cores(jnp.stack(gs))
        grad_others.append(other)
        shape = (samples, mode_dev, chans, 2 * width)
        (back,) = call(
            functools.partial(back_kernel, samples),
            (mode_dev,),
            [weight_half(part, False), weight_half(part, True), stacked(other), *[row_mode(g) for g in gs]],
            [(shape, BF, (samples, 1, chans, 2 * width), lambda i, *_: (0, i, 0, 0))],
            mix_flops,
            prefetch=core_ref,
        )
        back_parts += from_modes([back[j] for j in range(samples)], blocks)

    (spectral_grad,) = call(
        functools.partial(weight_kernel, samples, CHUNKS),
        (mode_dev,),
        [
            *[stacked(a) for a in grad_others],
            *[row_mode(x) for xs in field_modes for x in xs],
            *[row_mode(g) for gs in grad_modes for g in gs],
        ],
        [
            (
                (2, mode_dev, chans, 2 * half, freqs),
                BF,
                (2, 1, chans, 2 * half, freqs),
                lambda i, *_: (0, i, 0, 0, 0),
            )
        ],
        mix_flops * CHUNKS,
        prefetch=core_ref,
    )

    (sums,) = call(
        functools.partial(final_kernel, blocks, CHUNKS, unit_scale),
        (chans,),
        [
            (own_lw, None, None),
            whole(sample),
            channel(back_a),
            channel(back_b),
            whole(col_inv),
            whole(row_inv),
            *[channel(a) for a in back_parts],
        ],
        [((chans, inputs, 8, 128), F32, (1, inputs, 8, 128), lambda i, *_: (i, 0, 0, 0))],
        matrix,
        chans * rows * cells,
    )
    lift_own = all_sum(jnp.sum(sums, axis=(2, 3)).T * norm_scale, ("dp", "blk"))
    lift_other = swap_cores(lift_own)
    lift_grad = jnp.where(
        core == 0, jnp.concatenate([lift_own, lift_other], 1), jnp.concatenate([lift_other, lift_own], 1)
    )
    return (spectral_grad, local_grad, lift_grad)


def solution(mesh):
    in_specs = (
        P("dp", "parts", "blk", None),
        P("parts", None),
        P("parts", "chan"),
        P("parts", ("blk", "dp"), "chan", None, None),
        P("dp", "chan", "blk", "parts"),
    )
    out_specs = (
        P("parts", ("blk", "dp"), "chan", None, None),
        P("parts", "chan"),
        P("parts", None),
    )
    return jax.shard_map(per_device, mesh=mesh, in_specs=in_specs, out_specs=out_specs, check_vma=False)
```

```python
import functools
import math

import jax
import jax.numpy as jnp
import ml_dtypes
import numpy as np
from jax import lax
from jax.experimental import pallas as pl
from jax.experimental.pallas import tpu as pltpu
from jax.sharding import PartitionSpec as P

BF = jnp.bfloat16
F32 = jnp.float32
TWO_PI = 2.0 * math.pi
CHUNKS = 2
VMEM = 48 * 1024 * 1024


def table(freqs, points, length):
    product = (freqs % length)[:, None] * points[None, :] % length
    angle = np.float32(TWO_PI / length) * product.astype(np.float32)
    return np.cos(angle), np.sin(angle)


def column_table(cells, modes):
    cos, sin = table(np.arange(modes), np.arange(cells), cells)
    return np.ascontiguousarray(np.concatenate([cos, -sin], 0).T).astype(ml_dtypes.bfloat16)


def row_tables(rows, modes, blocks, samples):
    index = np.arange(modes)
    cos, sin = table(np.where(index < modes // 2, index, index - modes), np.arange(rows), rows)
    both = np.stack([cos, sin]).astype(ml_dtypes.bfloat16)
    sub = modes // (blocks * samples)
    piece = sub // CHUNKS
    local = rows // blocks
    out = np.empty((blocks, samples, 2 * modes, local), ml_dtypes.bfloat16)
    for z in range(blocks):
        part = both[:, :, z * local : (z + 1) * local]
        for s in range(samples):
            order = np.concatenate(
                [
                    np.arange(piece) + piece * c + sub * ((s ^ j) + samples * ((z + d) % blocks))
                    for d in range(blocks)
                    for c in range(CHUNKS)
                    for j in range(samples)
                ]
            )
            out[z, s] = part[:, order].reshape(2 * modes, local)
    return out


def gelu_slope(value):
    bell = jnp.exp(-0.5 * value * value)
    t = pl.reciprocal(1.0 + (0.3275911 / math.sqrt(2.0)) * jnp.abs(value))
    poly = 0.5 * 1.061405429
    for a in (-1.453152027, 1.421413741, -0.284496736, 0.254829592):
        poly = poly * t + 0.5 * a
    tail = poly * t * bell
    return jnp.where(value >= 0.0, 1.0 - tail, tail) + value * bell * (1.0 / math.sqrt(2.0 * math.pi))


def lift_rows(fields, lw, chan):
    total = fields[0] * lw[0, chan]
    for j in range(1, len(fields)):
        total = total + fields[j] * lw[j, chan]
    return jnp.tanh(total)


def row_forward(u, row_tab, scale):
    modes, width = row_tab.shape[0] // 2, u.shape[1] // 2
    prod = jnp.dot(row_tab, u, preferred_element_type=F32)
    real = (prod[:modes, :width] + prod[modes:, width:]) * scale
    imag = (prod[:modes, width:] - prod[modes:, :width]) * scale
    return jnp.concatenate([real.astype(BF), imag.astype(BF)], 1)


def split_modes(value, outs, at):
    rows = outs[0][0].shape[1]
    for c, part in enumerate(outs):
        for d, out in enumerate(part):
            lo = (d * len(outs) + c) * rows
            out[at] = value[lo : lo + rows]


def by_part(refs):
    each = len(refs) // CHUNKS
    return [refs[i * each : (i + 1) * each] for i in range(CHUNKS)]


def lift_kernel(scale, lw, fields, col, row_tab, lifted, *outs):
    group, rows, cells = lifted.shape
    first = pl.program_id(0) * group
    step = min(rows, 32)
    us = [[] for _ in range(group)]
    for lo in range(0, rows, step):
        f = [fields[j, lo : lo + step].astype(F32) for j in range(fields.shape[0])]
        for c in range(group):
            v = lift_rows(f, lw, first + c).astype(BF)
            lifted[c, lo : lo + step] = v
            us[c].append(jnp.dot(v, col[...], preferred_element_type=F32).astype(BF))
    for c in range(group):
        split_modes(row_forward(jnp.concatenate(us[c], 0), row_tab[...], scale), by_part(outs), c)


def slope_kernel(scale, first, lw, fields, col, row_tab, *refs):
    out, token = refs[-2:]
    inputs, rows, cells = fields.shape
    blocks, sub = out.shape[0], out.shape[3]
    chan = first + pl.program_id(0)
    step = min(rows, 32)
    us = [[] for _ in range(inputs)]
    for lo in range(0, rows, step):
        f = [fields[j, lo : lo + step].astype(F32) for j in range(inputs)]
        t = lift_rows(f, lw, chan)
        slope = 1.0 - t * t
        for j in range(inputs):
            us[j].append(jnp.dot((f[j] * slope).astype(BF), col[...], preferred_element_type=F32).astype(BF))
    for j in range(inputs):
        v = row_forward(jnp.concatenate(us[j], 0), row_tab[...], scale)
        for d in range(blocks):
            out[d, 0, j] = v[d * sub : (d + 1) * sub]
    token[...] = jnp.zeros(token.shape, F32)


def pair_kernel(low, high, f_low, f_high, out):
    for c in range(out.shape[0]):
        for j in range(out.shape[1]):
            total = None
            for b, f in ((low, f_low), (high, f_high)):
                prod = b[c].astype(F32) * f[0, c, j].astype(F32)
                for r in range(0, prod.shape[0], 8):
                    for k in range(0, prod.shape[1], 128):
                        tile = prod[r : r + 8, k : k + 128]
                        total = tile if total is None else total + tile
            out[c, j] = total


def own_pair_kernel(low, f_low, out):
    for c in range(out.shape[0]):
        for j in range(out.shape[1]):
            total = None
            prod = low[c].astype(F32) * f_low[0, c, j].astype(F32)
            for r in range(0, prod.shape[0], 8):
                for k in range(0, prod.shape[1], 128):
                    tile = prod[r : r + 8, k : k + 128]
                    total = tile if total is None else total + tile
            out[c, j] = total


def local_kernel(mix, own, other, out, token):
    n, rows, cells = own.shape
    for lo in range(0, cells, 256):
        at = pl.ds(lo, 256)
        both = jnp.concatenate([own[:, :, at].reshape(n * rows, 256), other[:, :, at].reshape(n * rows, 256)], 0)
        got = jnp.dot(mix[...], both, preferred_element_type=F32)
        out[:, :, at] = got.reshape(-1, rows, 256)
    token[...] = jnp.zeros(token.shape, F32)


def local_back_kernel(lw, mix, fields, own, other, grad, terms, sums):
    n, rows, cells = own.shape
    inputs = fields.shape[0]

    @pl.when(pl.program_id(0) == 0)
    def _():
        terms[...] = jnp.zeros(terms.shape, F32)
        sums[...] = jnp.zeros(sums.shape, F32)

    g = grad[...].reshape(-1, cells)
    for half, part in enumerate((own, other)):
        terms[half] += lax.dot_general(
            part[...].reshape(n * rows, cells), g, (((1,), (1,)), ((), ())), preferred_element_type=F32
        )

    def lanes(step, _):
        at = pl.ds(pl.multiple_of(step * 256, 256), 256)
        back = jnp.dot(mix[...], grad[:, :, at].reshape(-1, 256), preferred_element_type=F32)
        f = [fields[j, :, at].astype(F32) for j in range(inputs)]
        for c in range(2 * n):
            t = lift_rows(f, lw, c)
            total = back[c * rows : (c + 1) * rows] * (1.0 - t * t)
            for j in range(inputs):
                prod = f[j] * total
                prod = prod[:, :128] + prod[:, 128:]
                tile = prod[:8]
                for r in range(8, rows, 8):
                    tile = tile + prod[r : r + 8]
                sums[c, j] += tile
        return 0

    lax.fori_loop(0, cells // 256, lanes, 0)


def row_inverse(parts, row_inv):
    rows = row_inv.shape[0] // 2
    width = parts[0][0].shape[-1] // 2
    hops = (len(parts[0]) - 1) // 2
    blocks = [part[0][0] for part in parts]
    for s in range(hops - 1, -1, -1):
        blocks += [part[1 + s][0] + part[hops + hops - s][0] for part in parts]
    prod = jnp.dot(row_inv, jnp.concatenate(blocks, 0), preferred_element_type=F32)
    real = prod[:rows, :width] - prod[rows:, width:]
    imag = prod[:rows, width:] + prod[rows:, :width]
    return jnp.concatenate([real.astype(BF), imag.astype(BF)], 1)


def middle_kernel(blocks, grid_scale, scale, local, cotan, col, col_inv, row_tab, row_inv, *refs):
    n_in = CHUNKS * (2 * blocks - 1)
    grad, outs = refs[n_in], refs[n_in + 1 :]
    rows = grad.shape[1]
    h = row_inverse(by_part(refs[:n_in]), row_inv[...])
    step = min(rows, 32)
    pieces = []
    for lo in range(0, rows, step):
        grid = jnp.dot(h[lo : lo + step], col_inv[...], preferred_element_type=F32)
        pre = grid * grid_scale + local[0, lo : lo + step]
        g = (cotan[0, 0, lo : lo + step].astype(F32) * gelu_slope(pre)).astype(BF)
        grad[0, lo : lo + step] = g
        pieces.append(jnp.dot(g, col[...], preferred_element_type=F32).astype(BF))
    split_modes(row_forward(jnp.concatenate(pieces, 0), row_tab[...], scale), by_part(outs), 0)


def mix_kernel(samples, core, w_keep, w_send, *refs):
    xs, keep, send = refs[:samples], refs[samples], refs[samples + 1]
    width = w_keep.shape[-1]
    ins, outs = w_keep.shape[2], w_keep.shape[3]
    for lo in range(0, width, 128):
        re, im = pl.ds(lo, 128), pl.ds(width + lo, 128)
        xr = [x[0, :, re].astype(F32) for x in xs]
        xi = [x[0, :, im].astype(F32) for x in xs]
        for w, out in ((w_keep, keep), (w_send, send)):
            real = [jnp.zeros((outs, 128), F32) for _ in range(samples)]
            imag = [jnp.zeros((outs, 128), F32) for _ in range(samples)]
            for i in range(ins):
                wr = w[0, 0, i, :, re].astype(F32)
                wi = w[1, 0, i, :, re].astype(F32)
                for s in range(samples):
                    a, b = xr[s][i : i + 1], xi[s][i : i + 1]
                    real[s] = real[s] + (wr * a - wi * b)
                    imag[s] = imag[s] + (wr * b + wi * a)
            for s in range(samples):
                out[s, 0, :, re] = real[s].astype(BF)
                out[s, 0, :, im] = imag[s].astype(BF)


def back_kernel(samples, core, w_own, w_other, g_other, *refs):
    gs, out = refs[:samples], refs[samples]
    width = w_own.shape[-1]
    ins, outs = w_own.shape[2], w_own.shape[3]
    for lo in range(0, width, 128):
        re, im = pl.ds(lo, 128), pl.ds(width + lo, 128)
        gr = [[g[0, :, re].astype(F32) for g in gs], [g_other[s, 0, :, re].astype(F32) for s in range(samples)]]
        gi = [[g[0, :, im].astype(F32) for g in gs], [g_other[s, 0, :, im].astype(F32) for s in range(samples)]]
        real = [[] for _ in range(samples)]
        imag = [[] for _ in range(samples)]
        for i in range(ins):
            w = [
                (w_own[0, 0, i, :, re].astype(F32), w_own[1, 0, i, :, re].astype(F32)),
                (w_other[0, 0, i, :, re].astype(F32), w_other[1, 0, i, :, re].astype(F32)),
            ]
            for s in range(samples):
                r = m = None
                for half in range(2):
                    wr, wi = w[half]
                    a, b = gr[half][s], gi[half][s]
                    r1 = wr * a + wi * b
                    m1 = wr * b - wi * a
                    r, m = (r1, m1) if r is None else (r + r1, m + m1)
                real[s].append(jnp.sum(r, axis=0, keepdims=True))
                imag[s].append(jnp.sum(m, axis=0, keepdims=True))
        for s in range(samples):
            out[s, 0, :, re] = jnp.concatenate(real[s], 0).astype(BF)
            out[s, 0, :, im] = jnp.concatenate(imag[s], 0).astype(BF)


def weight_kernel(samples, core, *refs):
    g_other, out, token = refs[0], refs[-2], refs[-1]
    xs, gs = refs[1 : 1 + samples], refs[1 + samples : 1 + 2 * samples]
    ins, half = xs[0].shape[1], gs[0].shape[1]
    width = xs[0].shape[2] // 2
    own = pl.ds(pl.multiple_of(core[0] * half, half), half)
    other = pl.ds(pl.multiple_of((1 - core[0]) * half, half), half)
    for lo in range(0, width, 128):
        re, im = pl.ds(lo, 128), pl.ds(width + lo, 128)
        xr = [x[0, :, re].astype(F32) for x in xs]
        xi = [x[0, :, im].astype(F32) for x in xs]
        for where in (own, other):
            if where is own:
                gr = [g[0, :, re].astype(F32) for g in gs]
                gi = [g[0, :, im].astype(F32) for g in gs]
            else:
                gr = [g_other[s, 0, :, re].astype(F32) for s in range(samples)]
                gi = [g_other[s, 0, :, im].astype(F32) for s in range(samples)]
            for i in range(ins):
                real = imag = None
                for s in range(samples):
                    a, b = xr[s][i : i + 1], xi[s][i : i + 1]
                    r1 = gr[s] * a + gi[s] * b
                    m1 = gi[s] * a - gr[s] * b
                    real, imag = (r1, m1) if real is None else (real + r1, imag + m1)
                out[0, 0, i, where, re] = real.astype(BF)
                out[1, 0, i, where, re] = imag.astype(BF)
    token[...] = jnp.zeros(token.shape, F32)


TOKEN = ((8, 128), F32, (8, 128), lambda i, *_: (0, 0))


def call(body, grid, ins, outs, flops, transcendentals=0, prefetch=None, tokens=(), into=None):
    scalars = 0 if prefetch is None else 1

    def spec(block, index):
        if block is None:
            return pl.BlockSpec(memory_space=pltpu.SMEM)
        return pl.BlockSpec(block, index)

    moved = 0
    for a, block, _ in ins:
        moved += a.size * a.dtype.itemsize if block is None else math.prod(block) * math.prod(grid) * a.dtype.itemsize
    moved += sum(math.prod(b) * math.prod(grid) * jnp.dtype(t).itemsize for _, t, b, _ in outs)
    extra = list(tokens) + ([] if into is None else [into])

    def kernel(*refs):
        n = scalars + len(ins)
        body(*refs[:n], *refs[n + len(extra) :])

    return pl.pallas_call(
        kernel,
        grid_spec=pltpu.PrefetchScalarGridSpec(
            num_scalar_prefetch=scalars,
            grid=grid,
            in_specs=[spec(b, i) for _, b, i in ins] + [pl.BlockSpec(memory_space=pl.ANY)] * len(extra),
            out_specs=[spec(b, i) for _, _, b, i in outs],
        ),
        out_shape=[jax.ShapeDtypeStruct(s, t) for s, t, _, _ in outs],
        input_output_aliases={} if into is None else {scalars + len(ins) + len(extra) - 1: 0},
        compiler_params=pltpu.CompilerParams(vmem_limit_bytes=VMEM),
        cost_estimate=pl.CostEstimate(flops=int(flops), bytes_accessed=int(moved), transcendentals=int(transcendentals)),
    )(*(() if prefetch is None else (prefetch,)), *[a for a, _, _ in ins], *extra)


def hold(value, *tokens):
    if not tokens:
        return value
    anywhere = pl.BlockSpec(memory_space=pl.ANY)
    return pl.pallas_call(
        lambda *refs: None,
        in_specs=[anywhere] * (1 + len(tokens)),
        out_specs=anywhere,
        out_shape=jax.ShapeDtypeStruct(value.shape, value.dtype),
        input_output_aliases={0: 0},
        cost_estimate=pl.CostEstimate(flops=0, bytes_accessed=0, transcendentals=0),
    )(value, *tokens)


def add_kernel(a, b, c, d, up, down):
    up[...] = (a[...].astype(F32) + b[...].astype(F32)).astype(BF)
    down[...] = (c[...].astype(F32) + d[...].astype(F32)).astype(BF)


def add_pairs(a, b, c, d, tokens):
    n = a.shape[0] // 2
    part = ((n, *a.shape[1:]), lambda i, *_: (i, 0, 0))
    return call(
        add_kernel, (2,), [(v, *part) for v in (a, b, c, d)], [(a.shape, BF, *part)] * 2, 4 * a.size, tokens=tokens
    )


def chain_sum(parts, fill, start):
    hops = len(parts) - 1
    blocks = hops + 1
    below = above = None
    tokens = []
    for t in range(hops):
        up, down = parts[hops - t], parts[t + 1]
        if t:
            up, down = add_pairs(up, below, down, above, tokens)
        elif start:
            up, down = hold(up, *start), hold(down, *start)
        below = lax.ppermute(up, "blk", [(z, z + 1) for z in range(t + 1)])
        above = lax.ppermute(down, "blk", [(blocks - 1 - z, blocks - 2 - z) for z in range(t + 1)])
        tokens = [fill.pop(0)()] if fill else []
    return parts[0], below, above


def chain_gather(own, blocks):
    below, above = [], []
    up = down = own
    for t in range(blocks - 1):
        up = lax.ppermute(up, "blk", [(z, z + 1) for z in range(t, blocks - 1)])
        down = lax.ppermute(down, "blk", [(blocks - 1 - z, blocks - 2 - z) for z in range(t, blocks - 1)])
        below.append(up)
        above.append(down)
    return [own, *below, *above]


def swap_samples(pieces):
    n = len(pieces)
    return [pieces[0]] + [lax.ppermute(pieces[j], "dp", [(i, i ^ j) for i in range(n)]) for j in range(1, n)]


def swap_cores(value):
    return lax.ppermute(value, "chan", [(0, 1), (1, 0)])


def to_modes(shares, samples):
    own, below, above = shares
    total = (own.astype(F32) + below.astype(F32) + above.astype(F32)).astype(BF).transpose(1, 0, 2)
    sub = total.shape[0] // samples
    return swap_samples([total[j * sub : (j + 1) * sub] for j in range(samples)])


def from_modes(pieces, blocks):
    return chain_gather(jnp.concatenate(swap_samples(pieces), 0).transpose(1, 0, 2), blocks)


def all_sum(value, axes):
    for axis in axes:
        n = lax.axis_size(axis)
        step = 1
        while step < n:
            value = value + lax.ppermute(value, axis, [(i, i ^ step) for i in range(n)])
            step *= 2
    return value


def per_device(fields, lift_weight, local_weight, spectral_weight, cotangent):
    blocks = lax.axis_size("blk")
    samples = lax.axis_size("dp")
    sample = fields[0]
    inputs, rows, cells = sample.shape
    chans = cotangent.shape[1]
    mode_dev = spectral_weight.shape[1]
    half = spectral_weight.shape[3] // 2
    freqs = spectral_weight.shape[4]
    width = 2 * freqs
    modes = mode_dev * blocks * samples
    sub = modes // blocks
    piece = mode_dev // CHUNKS
    all_rows = rows * blocks
    z, s, core = lax.axis_index("blk"), lax.axis_index("dp"), lax.axis_index("chan")
    core_ref = core.astype(jnp.int32)[None]
    unit_scale = 1.0 / math.sqrt(all_rows * cells)
    norm_scale = 1.0 / math.sqrt(samples * all_rows * cells)

    col = jnp.asarray(column_table(cells, freqs))
    col_inv = jnp.asarray(np.ascontiguousarray(column_table(cells, freqs).T))
    row_tab = lax.dynamic_slice(
        jnp.asarray(row_tables(all_rows, modes, blocks, samples)), (z, s, 0, 0), (1, 1, 2 * modes, rows)
    )[0, 0]
    row_inv = row_tab.reshape(2, modes, rows).transpose(0, 2, 1).reshape(2 * rows, modes)
    lw_wide = lift_weight.astype(F32)
    own_lw = lax.dynamic_slice_in_dim(lw_wide, core * chans, chans, 1)
    both_lw = jnp.concatenate([own_lw, lax.dynamic_slice_in_dim(lw_wide, (1 - core) * chans, chans, 1)], 1)
    lw_rows = jnp.concatenate(
        [
            lax.dynamic_slice_in_dim(local_weight, core * chans, chans, 0),
            lax.dynamic_slice_in_dim(local_weight, (1 - core) * chans, chans, 0),
        ],
        0,
    )
    group_rows = 16
    eye = jnp.eye(group_rows, dtype=BF)
    spread = (lw_rows[:, None, :, None] * eye[None, :, None, :]).reshape(2 * chans * group_rows, chans * group_rows)

    def whole(a):
        return (a, a.shape, lambda i, *_: (0,) * a.ndim)

    def channel(a, n=1):
        return (a, (n, *a.shape[1:]), lambda i, *_: (i,) + (0,) * (a.ndim - 1))

    def part_outs(n):
        shape = (chans, sub // CHUNKS, width)
        return [(shape, BF, (n, *shape[1:]), lambda i, *_: (i, 0, 0)) for _ in range(CHUNKS * blocks)]

    matrix = chans * rows * 4 * freqs * (cells + 2 * modes)
    group = 2
    lifted, *shares = call(
        functools.partial(lift_kernel, unit_scale),
        (chans // group,),
        [(own_lw, None, None), whole(sample), whole(col), whole(row_tab)],
        [((chans, rows, cells), BF, (group, rows, cells), lambda i, *_: (i, 0, 0)), *part_outs(group)],
        matrix,
        chans * rows * cells,
    )
    shares = by_part(shares)
    lifted_other = swap_cores(lifted)

    slopes = [None]

    def slope_piece(first, count):
        def run():
            got, token = call(
                functools.partial(slope_kernel, unit_scale, first),
                (count,),
                [(own_lw, None, None), whole(sample), whole(col), whole(row_tab)],
                [
                    (
                        (blocks, chans, inputs, sub, width),
                        BF,
                        (blocks, 1, inputs, sub, width),
                        lambda i, *_, first=first: (0, first + i, 0, 0, 0),
                    ),
                    TOKEN,
                ],
                matrix * inputs * count // chans,
                count * rows * cells,
                tokens=() if slopes[0] is not None else (shares[0][0],),
                into=slopes[0],
            )
            slopes[0] = got
            return token

        return run

    locals_ = [None]

    def local_piece():
        got, token = call(
            local_kernel,
            (rows // group_rows,),
            [
                whole(spread.T),
                (lifted, (chans, group_rows, cells), lambda i, *_: (0, i, 0)),
                (lifted_other, (chans, group_rows, cells), lambda i, *_: (0, i, 0)),
            ],
            [((chans, rows, cells), F32, (chans, group_rows, cells), lambda i, *_: (0, i, 0)), TOKEN],
            4 * chans * chans * group_rows * rows * cells,
        )
        locals_[0] = got
        return token

    def weight_half(part, other):
        return (
            spectral_weight,
            (2, 1, chans, half, freqs),
            lambda i, c, part=part, other=other: (0, part * piece + i, 0, (1 - c[0]) if other else c[0], 0),
        )

    def row_mode(a):
        return (a, (1, *a.shape[1:]), lambda i, *_: (i, 0, 0))

    def stacked(a):
        return (a, (samples, 1, *a.shape[2:]), lambda i, *_: (0, i, 0, 0))

    def stack_out(n):
        return ((samples, piece, n, width), BF, (samples, 1, n, width), lambda i, *_: (0, i, 0, 0))

    mix_flops = 16 * samples * piece * chans * half * freqs
    count = -(-chans // 5)
    fill = [slope_piece(i, min(count, chans - i)) for i in range(0, chans, count)]
    fill.insert(3, local_piece)
    field_modes, out_parts = [], []
    previous = ()
    for part in range(CHUNKS):
        got = chain_sum(shares[part], fill, previous)
        previous = got[1:]
        xs = to_modes(got, samples)
        field_modes.append(xs)
        keep, send = call(
            functools.partial(mix_kernel, samples),
            (piece,),
            [weight_half(part, False), weight_half(part, True), *[row_mode(x) for x in xs]],
            [stack_out(half)] * 2,
            mix_flops,
            prefetch=core_ref,
        )
        total = (keep.astype(F32) + swap_cores(send).astype(F32)).astype(BF)
        out_parts += from_modes([total[j] for j in range(samples)], blocks)
    while fill:
        fill.pop(0)()
    slopes, local = slopes[0], locals_[0]

    grad_z, *shares = call(
        functools.partial(middle_kernel, blocks, 2.0 * unit_scale, 2.0 * unit_scale),
        (chans,),
        [
            channel(local),
            (cotangent, (1, 1, rows, cells), lambda i, *_: (0, i, 0, 0)),
            whole(col),
            whole(col_inv),
            whole(row_tab),
            whole(row_inv),
            *[channel(a) for a in out_parts],
        ],
        [((chans, rows, cells), BF, (1, rows, cells), lambda i, *_: (i, 0, 0)), *part_outs(1)],
        2 * matrix,
        3 * chans * rows * cells,
    )
    shares = by_part(shares)

    terms, local_sums = [], []

    def back_piece(first, count):
        at = lambda i, *_: (0, first + i, 0)

        def run():
            t, v = call(
                local_back_kernel,
                (count,),
                [
                    (both_lw, None, None),
                    whole(spread),
                    (sample, (inputs, group_rows, cells), at),
                    (lifted, (chans, group_rows, cells), at),
                    (lifted_other, (chans, group_rows, cells), at),
                    (grad_z, (chans, group_rows, cells), at),
                ],
                [
                    (
                        (2, chans * group_rows, chans * group_rows),
                        F32,
                        (2, chans * group_rows, chans * group_rows),
                        lambda i, *_: (0, 0, 0),
                    ),
                    ((2 * chans, inputs, 8, 128), F32, (2 * chans, inputs, 8, 128), lambda i, *_: (0, 0, 0, 0)),
                ],
                8 * chans * chans * group_rows * group_rows * count * cells,
                2 * chans * group_rows * count * cells,
            )
            terms.append(t)
            local_sums.append(v)
            return v

        return run

    steps = rows // group_rows
    count = -(-steps // 4)
    fill = [back_piece(i, min(count, steps - i)) for i in range(0, steps, count)]
    previous = ()
    grad_modes, grad_others, back_parts = [], [], []
    for part in range(CHUNKS):
        got = chain_sum(shares[part], fill, previous)
        previous = got[1:]
        gs = to_modes(got, samples)
        other = swap_cores(jnp.stack(gs))
        grad_modes.append(gs)
        grad_others.append(other)
        (back,) = call(
            functools.partial(back_kernel, samples),
            (piece,),
            [weight_half(part, False), weight_half(part, True), stacked(other), *[row_mode(g) for g in gs]],
            [stack_out(chans)],
            mix_flops,
            prefetch=core_ref,
        )
        back_parts.append(from_modes([back[j] for j in range(samples)], blocks))
    while fill:
        fill.pop(0)()

    term = sum(terms).reshape(2 * chans, group_rows, chans, group_rows)
    term = jnp.sum(term * jnp.eye(group_rows, dtype=F32)[None, :, None, :], axis=(1, 3))
    own_first = jnp.stack([term[:chans], term[chans:]])
    ordered = jnp.where(core == 0, own_first, own_first[::-1]).reshape(2 * chans, chans)
    local_grad = all_sum(ordered * norm_scale, ("dp", "blk"))

    spectral_grad, tokens = None, []
    for part in range(CHUNKS):
        spectral_grad, token = call(
            functools.partial(weight_kernel, samples),
            (piece,),
            [
                stacked(grad_others[part]),
                *[row_mode(x) for x in field_modes[part]],
                *[row_mode(g) for g in grad_modes[part]],
            ],
            [
                (
                    (2, mode_dev, chans, 2 * half, freqs),
                    BF,
                    (2, 1, chans, 2 * half, freqs),
                    lambda i, *_, part=part: (0, part * piece + i, 0, 0, 0),
                ),
                TOKEN,
            ],
            mix_flops,
            prefetch=core_ref,
            into=spectral_grad,
        )
        tokens.append(token)

    sums = []
    bunch = 4
    for part in range(CHUNKS):
        own, arrived = back_parts[part][0], back_parts[part][1:]
        hops = blocks - 1
        out = [((chans, inputs, 8, 128), F32, (bunch, inputs, 8, 128), lambda i, *_: (i, 0, 0, 0))]

        def spectra(d, part=part):
            return (
                slopes,
                (1, bunch, inputs, sub // CHUNKS, width),
                lambda i, *_, d=d, part=part: (d, i, 0, part, 0),
            )

        flops = 4 * chans * inputs * sub * width // CHUNKS
        sums += call(own_pair_kernel, (chans // bunch,), [channel(own, bunch), spectra(0)], out, flops)
        for t in range(hops):
            last = part == CHUNKS - 1 and t == hops - 1
            sums += call(
                pair_kernel,
                (chans // bunch,),
                [
                    channel(arrived[t], bunch),
                    channel(arrived[hops + t], bunch),
                    spectra(blocks - 1 - t),
                    spectra(1 + t),
                ],
                out,
                2 * flops,
                tokens=tokens if last else (),
            )
    lift_own = jnp.sum(sum(sums), axis=(2, 3)).T
    lift_local = jnp.sum(sum(local_sums), axis=(2, 3)).T
    lift_own = jnp.concatenate([lift_own + lift_local[:, :chans], lift_local[:, chans:]], 1) * norm_scale
    lift_own = all_sum(lift_own, ("dp", "blk"))
    theirs = swap_cores(lift_own)
    mine = lift_own[:, :chans] + theirs[:, chans:]
    his = lift_own[:, chans:] + theirs[:, :chans]
    lift_grad = jnp.where(core == 0, jnp.concatenate([mine, his], 1), jnp.concatenate([his, mine], 1))
    return (spectral_grad, local_grad, lift_grad)


def solution(mesh):
    in_specs = (
        P("dp", "parts", "blk", None),
        P("parts", None),
        P("parts", "chan"),
        P("parts", ("blk", "dp"), "chan", None, None),
        P("dp", "chan", "blk", "parts"),
    )
    out_specs = (
        P("parts", ("blk", "dp"), "chan", None, None),
        P("parts", "chan"),
        P("parts", None),
    )
    return jax.shard_map(per_device, mesh=mesh, in_specs=in_specs, out_specs=out_specs, check_vma=False)
```

```python
import functools
import math

import jax
import jax.numpy as jnp
import ml_dtypes
import numpy as np
from jax import lax
from jax.experimental import pallas as pl
from jax.experimental.pallas import tpu as pltpu
from jax.sharding import PartitionSpec as P

BF = jnp.bfloat16
F32 = jnp.float32
TWO_PI = 2.0 * math.pi
CHUNKS = 1
VMEM = 48 * 1024 * 1024


def table(freqs, points, length):
    product = (freqs % length)[:, None] * points[None, :] % length
    angle = np.float32(TWO_PI / length) * product.astype(np.float32)
    return np.cos(angle), np.sin(angle)


def column_table(cells, modes):
    cos, sin = table(np.arange(modes), np.arange(cells), cells)
    return np.ascontiguousarray(np.concatenate([cos, -sin], 0).T).astype(ml_dtypes.bfloat16)


def row_tables(rows, modes, blocks, samples):
    index = np.arange(modes)
    cos, sin = table(np.where(index < modes // 2, index, index - modes), np.arange(rows), rows)
    both = np.stack([cos, sin]).astype(ml_dtypes.bfloat16)
    sub = modes // (blocks * samples)
    piece = sub // CHUNKS
    local = rows // blocks
    out = np.empty((blocks, samples, 2 * modes, local), ml_dtypes.bfloat16)
    for z in range(blocks):
        part = both[:, :, z * local : (z + 1) * local]
        for s in range(samples):
            order = np.concatenate(
                [
                    np.arange(piece) + piece * c + sub * ((s ^ j) + samples * ((z + d) % blocks))
                    for d in range(blocks)
                    for c in range(CHUNKS)
                    for j in range(samples)
                ]
            )
            out[z, s] = part[:, order].reshape(2 * modes, local)
    return out


def gelu_slope(value):
    return 0.5 * (1.0 + lax.erf(value * (1.0 / math.sqrt(2.0)))) + value * jnp.exp(-0.5 * value * value) * (
        1.0 / math.sqrt(2.0 * math.pi)
    )


def lift_rows(fields, lw, chan):
    total = fields[0] * lw[0, chan]
    for j in range(1, len(fields)):
        total = total + fields[j] * lw[j, chan]
    return jnp.tanh(total)


def row_forward(u, row_tab, scale):
    modes, width = row_tab.shape[0] // 2, u.shape[1] // 2
    prod = jnp.dot(row_tab, u, preferred_element_type=F32)
    real = (prod[:modes, :width] + prod[modes:, width:]) * scale
    imag = (prod[:modes, width:] - prod[modes:, :width]) * scale
    return jnp.concatenate([real.astype(BF), imag.astype(BF)], 1)


def split_modes(value, outs, at):
    rows = outs[0][0].shape[1]
    for c, part in enumerate(outs):
        for d, out in enumerate(part):
            lo = (d * len(outs) + c) * rows
            out[at] = value[lo : lo + rows]


def by_part(refs):
    each = len(refs) // CHUNKS
    return [refs[i * each : (i + 1) * each] for i in range(CHUNKS)]


def lift_kernel(bunch, scale, lw, fields, col, row_tab, lifted, *outs):
    group, rows, cells = lifted.shape
    first = pl.program_id(0) * group
    lanes = min(cells, 512)
    for b in range(0, group, bunch):
        for lo in range(0, rows, 16):
            for at in range(0, cells, lanes):
                f = [fields[j, lo : lo + 16, at : at + lanes].astype(F32) for j in range(fields.shape[0])]
                for c in range(b, b + bunch):
                    lifted[c, lo : lo + 16, at : at + lanes] = lift_rows(f, lw, first + c).astype(BF)
        u = jnp.dot(lifted[b : b + bunch].reshape(bunch * rows, cells), col[...], preferred_element_type=F32).astype(BF)
        for c in range(bunch):
            split_modes(row_forward(u[c * rows : (c + 1) * rows], row_tab[...], scale), by_part(outs), b + c)


def slope_kernel(scale, first, lw, fields, col, row_tab, *refs):
    out, token = refs[-2:]
    inputs, rows, cells = fields.shape
    blocks, group, sub = out.shape[0], out.shape[1], out.shape[3]
    for c in range(group):
        chan = first + pl.program_id(0) * group + c
        w = [[] for _ in range(inputs)]
        for lo in range(0, rows, 16):
            f = [fields[j, lo : lo + 16].astype(F32) for j in range(inputs)]
            t = lift_rows(f, lw, chan)
            slope = 1.0 - t * t
            for j in range(inputs):
                w[j].append((f[j] * slope).astype(BF))
        u = jnp.dot(jnp.concatenate(sum(w, []), 0), col[...], preferred_element_type=F32).astype(BF)
        for j in range(inputs):
            v = row_forward(u[j * rows : (j + 1) * rows], row_tab[...], scale)
            for d in range(blocks):
                out[d, c, j] = v[d * sub : (d + 1) * sub]
    token[...] = jnp.zeros(token.shape, F32)


def pair_kernel(n, *refs):
    out, token = refs[-2:]
    for c in range(out.shape[0]):
        back = [b[c].astype(F32) for b in refs[:n]]
        for j in range(out.shape[1]):
            total = None
            for b, f in zip(back, refs[n : 2 * n], strict=True):
                for r in range(0, b.shape[0], 8):
                    prod = b[r : r + 8] * f[0, c, j, r : r + 8].astype(F32)
                    total = prod if total is None else total + prod
            tile = total[:, :128]
            for k in range(128, total.shape[1], 128):
                tile = tile + total[:, k : k + 128]
            out[c, j] = tile
    token[...] = jnp.zeros(token.shape, F32)


def local_kernel(mix, own, other, out, token):
    n, rows, cells = own.shape
    for lo in range(0, cells, 256):
        at = pl.ds(lo, 256)
        both = jnp.concatenate([own[:, :, at].reshape(n * rows, 256), other[:, :, at].reshape(n * rows, 256)], 0)
        got = jnp.dot(mix[...], both, preferred_element_type=F32)
        out[:, :, at] = got.reshape(-1, rows, 256)
    token[...] = jnp.zeros(token.shape, F32)


def local_back_kernel(lw, mix, fields, own, other, grad, terms, sums):
    n, rows, cells = own.shape
    inputs = fields.shape[0]

    @pl.when(pl.program_id(0) == 0)
    def _():
        terms[...] = jnp.zeros(terms.shape, F32)
        sums[...] = jnp.zeros(sums.shape, F32)

    g = grad[...].reshape(-1, cells)
    for half, part in enumerate((own, other)):
        terms[half] += lax.dot_general(
            part[...].reshape(n * rows, cells), g, (((1,), (1,)), ((), ())), preferred_element_type=F32
        )

    def lanes(step, _):
        at = pl.ds(pl.multiple_of(step * 256, 256), 256)
        back = jnp.dot(mix[...], grad[:, :, at].reshape(-1, 256), preferred_element_type=F32)
        f = [fields[j, :, at].astype(F32) for j in range(inputs)]
        for c in range(2 * n):
            t = lift_rows(f, lw, c)
            total = back[c * rows : (c + 1) * rows] * (1.0 - t * t)
            for j in range(inputs):
                prod = f[j] * total
                prod = prod[:, :128] + prod[:, 128:]
                tile = prod[:8]
                for r in range(8, rows, 8):
                    tile = tile + prod[r : r + 8]
                sums[c, j] += tile
        return 0

    lax.fori_loop(0, cells // 256, lanes, 0)


def row_inverse(parts, chan, row_inv):
    rows = row_inv.shape[0] // 2
    width = parts[0][0].shape[-1] // 2
    hops = (len(parts[0]) - 1) // 2
    blocks = [part[0][chan] for part in parts]
    for s in range(hops - 1, -1, -1):
        blocks += [part[1 + s][chan] + part[hops + hops - s][chan] for part in parts]
    prod = jnp.dot(row_inv, jnp.concatenate(blocks, 0), preferred_element_type=F32)
    real = prod[:rows, :width] - prod[rows:, width:]
    imag = prod[:rows, width:] + prod[rows:, :width]
    return jnp.concatenate([real.astype(BF), imag.astype(BF)], 1)


def middle_kernel(blocks, bunch, grid_scale, scale, local, cotan, col, col_inv, row_tab, row_inv, *refs):
    n_in = CHUNKS * (2 * blocks - 1)
    parts, grad, outs = by_part(refs[:n_in]), refs[n_in], refs[n_in + 1 :]
    group, rows, cells = grad.shape
    for b in range(0, group, bunch):
        h = jnp.concatenate([row_inverse(parts, c, row_inv[...]) for c in range(b, b + bunch)], 0)
        grid = jnp.dot(h, col_inv[...], preferred_element_type=F32)
        for c in range(bunch):
            for lo in range(0, rows, 16):
                pre = grid[c * rows + lo : c * rows + lo + 16] * grid_scale + local[b + c, lo : lo + 16]
                slope = cotan[0, b + c, lo : lo + 16].astype(F32) * gelu_slope(pre)
                grad[b + c, lo : lo + 16] = slope.astype(BF)
        u = jnp.dot(grad[b : b + bunch].reshape(bunch * rows, cells), col[...], preferred_element_type=F32).astype(BF)
        for c in range(bunch):
            split_modes(row_forward(u[c * rows : (c + 1) * rows], row_tab[...], scale), by_part(outs), b + c)


def mix_kernel(samples, core, w_keep, w_send, *refs):
    xs, keep, send = refs[:samples], refs[samples], refs[samples + 1]
    width = w_keep.shape[-1]
    ins, outs = w_keep.shape[2], w_keep.shape[3]
    for lo in range(0, width, 128):
        re, im = pl.ds(lo, 128), pl.ds(width + lo, 128)
        xr = [x[0, :, re].astype(F32) for x in xs]
        xi = [x[0, :, im].astype(F32) for x in xs]
        for w, out in ((w_keep, keep), (w_send, send)):
            real = [jnp.zeros((outs, 128), F32) for _ in range(samples)]
            imag = [jnp.zeros((outs, 128), F32) for _ in range(samples)]
            for i in range(ins):
                wr = w[0, 0, i, :, re].astype(F32)
                wi = w[1, 0, i, :, re].astype(F32)
                for s in range(samples):
                    a, b = xr[s][i : i + 1], xi[s][i : i + 1]
                    real[s] = real[s] + (wr * a - wi * b)
                    imag[s] = imag[s] + (wr * b + wi * a)
            for s in range(samples):
                out[s, 0, :, re] = real[s].astype(BF)
                out[s, 0, :, im] = imag[s].astype(BF)


def back_kernel(samples, core, w_own, w_other, g_other, *refs):
    gs, out = refs[:samples], refs[samples]
    width = w_own.shape[-1]
    ins, outs = w_own.shape[2], w_own.shape[3]
    for lo in range(0, width, 128):
        re, im = pl.ds(lo, 128), pl.ds(width + lo, 128)
        gr = [[g[0, :, re].astype(F32) for g in gs], [g_other[s, 0, :, re].astype(F32) for s in range(samples)]]
        gi = [[g[0, :, im].astype(F32) for g in gs], [g_other[s, 0, :, im].astype(F32) for s in range(samples)]]
        real = [[] for _ in range(samples)]
        imag = [[] for _ in range(samples)]
        for i in range(ins):
            w = [
                (w_own[0, 0, i, :, re].astype(F32), w_own[1, 0, i, :, re].astype(F32)),
                (w_other[0, 0, i, :, re].astype(F32), w_other[1, 0, i, :, re].astype(F32)),
            ]
            for s in range(samples):
                r = m = None
                for half in range(2):
                    wr, wi = w[half]
                    a, b = gr[half][s], gi[half][s]
                    r1 = wr * a + wi * b
                    m1 = wr * b - wi * a
                    r, m = (r1, m1) if r is None else (r + r1, m + m1)
                real[s].append(jnp.sum(r, axis=0, keepdims=True))
                imag[s].append(jnp.sum(m, axis=0, keepdims=True))
        for s in range(samples):
            out[s, 0, :, re] = jnp.concatenate(real[s], 0).astype(BF)
            out[s, 0, :, im] = jnp.concatenate(imag[s], 0).astype(BF)


def weight_kernel(samples, core, *refs):
    g_other, out, token = refs[0], refs[-2], refs[-1]
    xs, gs = refs[1 : 1 + samples], refs[1 + samples : 1 + 2 * samples]
    ins, half = xs[0].shape[1], gs[0].shape[1]
    width = xs[0].shape[2] // 2
    own = pl.ds(pl.multiple_of(core[0] * half, half), half)
    other = pl.ds(pl.multiple_of((1 - core[0]) * half, half), half)
    for lo in range(0, width, 128):
        re, im = pl.ds(lo, 128), pl.ds(width + lo, 128)
        xr = [x[0, :, re].astype(F32) for x in xs]
        xi = [x[0, :, im].astype(F32) for x in xs]
        for where in (own, other):
            if where is own:
                gr = [g[0, :, re].astype(F32) for g in gs]
                gi = [g[0, :, im].astype(F32) for g in gs]
            else:
                gr = [g_other[s, 0, :, re].astype(F32) for s in range(samples)]
                gi = [g_other[s, 0, :, im].astype(F32) for s in range(samples)]
            for i in range(ins):
                real = imag = None
                for s in range(samples):
                    a, b = xr[s][i : i + 1], xi[s][i : i + 1]
                    r1 = gr[s] * a + gi[s] * b
                    m1 = gi[s] * a - gr[s] * b
                    real, imag = (r1, m1) if real is None else (real + r1, imag + m1)
                out[0, 0, i, where, re] = real.astype(BF)
                out[1, 0, i, where, re] = imag.astype(BF)
    token[...] = jnp.zeros(token.shape, F32)


TOKEN = ((8, 128), F32, (8, 128), lambda i, *_: (0, 0))


def call(body, grid, ins, outs, flops, transcendentals=0, prefetch=None, tokens=(), into=None):
    scalars = 0 if prefetch is None else 1

    def spec(block, index):
        if block is None:
            return pl.BlockSpec(memory_space=pltpu.SMEM)
        return pl.BlockSpec(block, index)

    moved = 0
    for a, block, _ in ins:
        moved += a.size * a.dtype.itemsize if block is None else math.prod(block) * math.prod(grid) * a.dtype.itemsize
    moved += sum(math.prod(b) * math.prod(grid) * jnp.dtype(t).itemsize for _, t, b, _ in outs)
    extra = list(tokens) + ([] if into is None else [into])

    def kernel(*refs):
        n = scalars + len(ins)
        body(*refs[:n], *refs[n + len(extra) :])

    return pl.pallas_call(
        kernel,
        grid_spec=pltpu.PrefetchScalarGridSpec(
            num_scalar_prefetch=scalars,
            grid=grid,
            in_specs=[spec(b, i) for _, b, i in ins] + [pl.BlockSpec(memory_space=pl.ANY)] * len(extra),
            out_specs=[spec(b, i) for _, _, b, i in outs],
        ),
        out_shape=[jax.ShapeDtypeStruct(s, t) for s, t, _, _ in outs],
        input_output_aliases={} if into is None else {scalars + len(ins) + len(extra) - 1: 0},
        compiler_params=pltpu.CompilerParams(vmem_limit_bytes=VMEM),
        cost_estimate=pl.CostEstimate(flops=int(flops), bytes_accessed=int(moved), transcendentals=int(transcendentals)),
    )(*(() if prefetch is None else (prefetch,)), *[a for a, _, _ in ins], *extra)


def hold(value, *tokens):
    if not tokens:
        return value
    anywhere = pl.BlockSpec(memory_space=pl.ANY)
    return pl.pallas_call(
        lambda *refs: None,
        in_specs=[anywhere] * (1 + len(tokens)),
        out_specs=anywhere,
        out_shape=jax.ShapeDtypeStruct(value.shape, value.dtype),
        input_output_aliases={0: 0},
        cost_estimate=pl.CostEstimate(flops=0, bytes_accessed=0, transcendentals=0),
    )(value, *tokens)


def add_kernel(a, b, c, d, up, down):
    up[...] = (a[...].astype(F32) + b[...].astype(F32)).astype(BF)
    down[...] = (c[...].astype(F32) + d[...].astype(F32)).astype(BF)


def add_pairs(a, b, c, d, tokens):
    n = a.shape[0] // 2
    part = ((n, *a.shape[1:]), lambda i, *_: (i, 0, 0))
    return call(
        add_kernel, (2,), [(v, *part) for v in (a, b, c, d)], [(a.shape, BF, *part)] * 2, 4 * a.size, tokens=tokens
    )


def run_next(fill, source):
    return fill.pop(0)(source) if fill else None


def chain_sums(shares, fill):
    hops = len(shares[0]) - 1
    blocks = hops + 1
    got = [None] * len(shares)
    token = None
    for t in range(hops):
        for p, part in enumerate(shares):
            up, down = part[hops - t], part[t + 1]
            if t:
                up, down = add_pairs(up, got[p][1], down, got[p][2], [] if token is None else [token])
            elif token is not None:
                up, down = hold(up, token), hold(down, token)
            below = lax.ppermute(up, "blk", [(z, z + 1) for z in range(t + 1)])
            above = lax.ppermute(down, "blk", [(blocks - 1 - z, blocks - 2 - z) for z in range(t + 1)])
            got[p] = (part[0], below, above)
            token = run_next(fill, up)
    return got, token


def chain_gathers(owns, blocks, below, above, fill):
    token = None
    for t in range(blocks - 1):
        for p, own in enumerate(owns):
            if t and token is not None:
                below[p][-1], above[p][-1] = hold(below[p][-1], token), hold(above[p][-1], token)
            elif token is not None:
                own = hold(own, token)
                owns[p] = own
            up, down = (below[p][-1], above[p][-1]) if t else (own, own)
            below[p].append(lax.ppermute(up, "blk", [(z, z + 1) for z in range(t, blocks - 1)]))
            above[p].append(
                lax.ppermute(down, "blk", [(blocks - 1 - z, blocks - 2 - z) for z in range(t, blocks - 1)])
            )
            token = run_next(fill, up)
    return token


def swap_samples(pieces):
    n = len(pieces)
    return [pieces[0]] + [lax.ppermute(pieces[j], "dp", [(i, i ^ j) for i in range(n)]) for j in range(1, n)]


def swap_cores(value):
    return lax.ppermute(value, "chan", [(0, 1), (1, 0)])


def to_modes(shares, samples, token):
    own, below, above = shares
    if token is not None:
        own = hold(own, token)
    total = (own.astype(F32) + below.astype(F32) + above.astype(F32)).astype(BF).transpose(1, 0, 2)
    sub = total.shape[0] // samples
    return swap_samples([total[j * sub : (j + 1) * sub] for j in range(samples)])


def from_modes(pieces):
    return jnp.concatenate(swap_samples(pieces), 0).transpose(1, 0, 2)


def all_sum(value, axes):
    for axis in axes:
        n = lax.axis_size(axis)
        step = 1
        while step < n:
            value = value + lax.ppermute(value, axis, [(i, i ^ step) for i in range(n)])
            step *= 2
    return value


def per_device(fields, lift_weight, local_weight, spectral_weight, cotangent):
    blocks = lax.axis_size("blk")
    samples = lax.axis_size("dp")
    sample = fields[0]
    inputs, rows, cells = sample.shape
    chans = cotangent.shape[1]
    mode_dev = spectral_weight.shape[1]
    half = spectral_weight.shape[3] // 2
    freqs = spectral_weight.shape[4]
    width = 2 * freqs
    modes = mode_dev * blocks * samples
    sub = modes // blocks
    piece = mode_dev // CHUNKS
    all_rows = rows * blocks
    z, s, core = lax.axis_index("blk"), lax.axis_index("dp"), lax.axis_index("chan")
    core_ref = core.astype(jnp.int32)[None]
    unit_scale = 1.0 / math.sqrt(all_rows * cells)
    norm_scale = 1.0 / math.sqrt(samples * all_rows * cells)

    col = jnp.asarray(column_table(cells, freqs))
    col_inv = jnp.asarray(np.ascontiguousarray(column_table(cells, freqs).T))
    row_tab = lax.dynamic_slice(
        jnp.asarray(row_tables(all_rows, modes, blocks, samples)), (z, s, 0, 0), (1, 1, 2 * modes, rows)
    )[0, 0]
    row_inv = row_tab.reshape(2, modes, rows).transpose(0, 2, 1).reshape(2 * rows, modes)
    lw_wide = lift_weight.astype(F32)
    own_lw = lax.dynamic_slice_in_dim(lw_wide, core * chans, chans, 1)
    both_lw = jnp.concatenate([own_lw, lax.dynamic_slice_in_dim(lw_wide, (1 - core) * chans, chans, 1)], 1)
    lw_rows = jnp.concatenate(
        [
            lax.dynamic_slice_in_dim(local_weight, core * chans, chans, 0),
            lax.dynamic_slice_in_dim(local_weight, (1 - core) * chans, chans, 0),
        ],
        0,
    )
    group_rows = 16
    eye = jnp.eye(group_rows, dtype=BF)
    spread = (lw_rows[:, None, :, None] * eye[None, :, None, :]).reshape(2 * chans * group_rows, chans * group_rows)

    def whole(a):
        return (a, a.shape, lambda i, *_: (0,) * a.ndim)

    def channel(a, n=1):
        return (a, (n, *a.shape[1:]), lambda i, *_: (i,) + (0,) * (a.ndim - 1))

    def part_outs(n):
        shape = (chans, sub // CHUNKS, width)
        return [(shape, BF, (n, *shape[1:]), lambda i, *_: (i, 0, 0)) for _ in range(CHUNKS * blocks)]

    matrix = chans * rows * 4 * freqs * (cells + 2 * modes)
    group, bunch = math.gcd(chans, 8), math.gcd(chans, 4)
    lifted, *shares = call(
        functools.partial(lift_kernel, bunch, unit_scale),
        (chans // group,),
        [(own_lw, None, None), whole(sample), whole(col), whole(row_tab)],
        [((chans, rows, cells), BF, (group, rows, cells), lambda i, *_: (i, 0, 0)), *part_outs(group)],
        matrix,
        chans * rows * cells,
    )
    shares = by_part(shares)
    lifted_other = swap_cores(lifted)

    slopes = [None]

    def slope_piece(first, count):
        def run(source):
            got, token = call(
                functools.partial(slope_kernel, unit_scale, first),
                (count // 2,),
                [(own_lw, None, None), whole(sample), whole(col), whole(row_tab)],
                [
                    (
                        (blocks, chans, inputs, sub, width),
                        BF,
                        (blocks, 2, inputs, sub, width),
                        lambda i, *_, first=first: (0, first // 2 + i, 0, 0, 0),
                    ),
                    TOKEN,
                ],
                matrix * inputs * count // chans,
                count * rows * cells,
                tokens=(source,),
                into=slopes[0],
            )
            slopes[0] = got
            return token

        return run

    locals_ = [None]

    def local_piece(first, count):
        def run(source):
            at = lambda i, *_: (0, first + i, 0)
            locals_[0], token = call(
                local_kernel,
                (count,),
                [
                    whole(spread.T),
                    (lifted, (chans, group_rows, cells), at),
                    (lifted_other, (chans, group_rows, cells), at),
                ],
                [((chans, rows, cells), F32, (chans, group_rows, cells), at), TOKEN],
                4 * chans * chans * group_rows * group_rows * count * cells,
                tokens=(source,),
                into=locals_[0],
            )
            return token

        return run

    def weight_half(part, other):
        return (
            spectral_weight,
            (2, 1, chans, half, freqs),
            lambda i, c, part=part, other=other: (0, part * piece + i, 0, (1 - c[0]) if other else c[0], 0),
        )

    def row_mode(a):
        return (a, (1, *a.shape[1:]), lambda i, *_: (i, 0, 0))

    def stacked(a):
        return (a, (samples, 1, *a.shape[2:]), lambda i, *_: (0, i, 0, 0))

    def stack_out(n):
        return ((samples, piece, n, width), BF, (samples, 1, n, width), lambda i, *_: (0, i, 0, 0))

    mix_flops = 16 * samples * piece * chans * half * freqs
    count = chans // 2
    fill = [slope_piece(i, count) for i in range(0, chans, count)]
    field_modes, out_parts, sent = [], [], []

    got, token = chain_sums(shares, fill)
    for run in fill:
        token = run(shares[0][0])
    for part in range(CHUNKS):
        xs = to_modes(got[part], samples, token)
        field_modes.append(xs)
        keep, send = call(
            functools.partial(mix_kernel, samples),
            (piece,),
            [weight_half(part, False), weight_half(part, True), *[row_mode(x) for x in xs]],
            [stack_out(half)] * 2,
            mix_flops,
            prefetch=core_ref,
            tokens=sent[-1:],
        )
        token = keep
        total = (keep.astype(F32) + swap_cores(send).astype(F32)).astype(BF)
        sent.append(from_modes([total[j] for j in range(samples)]))
    steps = rows // group_rows
    count = -(-steps // 2)
    fill = [local_piece(i, min(count, steps - i)) for i in range(0, steps, count)]
    below, above = [[] for _ in range(CHUNKS)], [[] for _ in range(CHUNKS)]
    chain_gathers(sent, blocks, below, above, fill)
    for part in range(CHUNKS):
        out_parts += [sent[part], *below[part], *above[part]]
    for run in fill:
        run(sent[-1])
    slopes, local = slopes[0], locals_[0]

    grad_z, *shares = call(
        functools.partial(middle_kernel, blocks, math.gcd(chans, 2), 2.0 * unit_scale, 2.0 * unit_scale),
        (chans // bunch,),
        [
            channel(local, bunch),
            (cotangent, (1, bunch, rows, cells), lambda i, *_: (0, i, 0, 0)),
            whole(col),
            whole(col_inv),
            whole(row_tab),
            whole(row_inv),
            *[channel(a, bunch) for a in out_parts],
        ],
        [((chans, rows, cells), BF, (bunch, rows, cells), lambda i, *_: (i, 0, 0)), *part_outs(bunch)],
        2 * matrix,
        3 * chans * rows * cells,
    )
    shares = by_part(shares)

    terms, local_sums = [], []

    def back_piece(first, count):
        at = lambda i, *_: (0, first + i, 0)

        def run(source):
            t, v = call(
                local_back_kernel,
                (count,),
                [
                    (both_lw, None, None),
                    whole(spread),
                    (sample, (inputs, group_rows, cells), at),
                    (lifted, (chans, group_rows, cells), at),
                    (lifted_other, (chans, group_rows, cells), at),
                    (grad_z, (chans, group_rows, cells), at),
                ],
                [
                    (
                        (2, chans * group_rows, chans * group_rows),
                        F32,
                        (2, chans * group_rows, chans * group_rows),
                        lambda i, *_: (0, 0, 0),
                    ),
                    ((2 * chans, inputs, 8, 128), F32, (2 * chans, inputs, 8, 128), lambda i, *_: (0, 0, 0, 0)),
                ],
                8 * chans * chans * group_rows * group_rows * count * cells,
                2 * chans * group_rows * count * cells,
                tokens=(source,),
            )
            terms.append(t)
            local_sums.append(v)
            return v

        return run

    steps = rows // group_rows
    count = -(-steps // 2)
    fill = [back_piece(i, min(count, steps - i)) for i in range(0, steps, count)]
    grad_modes, grad_others, sent = [], [], []

    got, token = chain_sums(shares, fill)
    for run in fill:
        token = run(grad_z)
    for part in range(CHUNKS):
        gs = to_modes(got[part], samples, token)
        other = swap_cores(jnp.stack(gs))
        grad_modes.append(gs)
        grad_others.append(other)
        (back,) = call(
            functools.partial(back_kernel, samples),
            (piece,),
            [weight_half(part, False), weight_half(part, True), stacked(other), *[row_mode(g) for g in gs]],
            [stack_out(chans)],
            mix_flops,
            prefetch=core_ref,
            tokens=sent[-1:],
        )
        token = back
        sent.append(from_modes([back[j] for j in range(samples)]))

    term = sum(terms).reshape(2 * chans, group_rows, chans, group_rows)
    term = jnp.sum(term * jnp.eye(group_rows, dtype=F32)[None, :, None, :], axis=(1, 3))
    own_first = jnp.stack([term[:chans], term[chans:]])
    ordered = jnp.where(core == 0, own_first, own_first[::-1]).reshape(2 * chans, chans)
    ordered = ordered * norm_scale

    gradient = [None]

    def weight_piece(part):
        def run(source):
            gradient[0], token = call(
                functools.partial(weight_kernel, samples),
                (piece,),
                [
                    stacked(grad_others[part]),
                    *[row_mode(x) for x in field_modes[part]],
                    *[row_mode(g) for g in grad_modes[part]],
                ],
                [
                    (
                        (2, mode_dev, chans, 2 * half, freqs),
                        BF,
                        (2, 1, chans, 2 * half, freqs),
                        lambda i, *_: (0, part * piece + i, 0, 0, 0),
                    ),
                    TOKEN,
                ],
                mix_flops,
                prefetch=core_ref,
                tokens=(source,),
                into=gradient[0],
            )
            return token

        return run

    sums = []
    at_once = 4

    def pairs(modes_of, tokens=()):
        def spectra(part, d):
            return (
                slopes,
                (1, at_once, inputs, sub // CHUNKS, width),
                lambda i, *_: (d, i, 0, part, 0),
            )

        got, token = call(
            functools.partial(pair_kernel, len(modes_of)),
            (chans // at_once,),
            [channel(a, at_once) for *_, a in modes_of] + [spectra(p, d) for p, d, _ in modes_of],
            [((chans, inputs, 8, 128), F32, (at_once, inputs, 8, 128), lambda i, *_: (i, 0, 0, 0)), TOKEN],
            4 * len(modes_of) * chans * inputs * sub * width // CHUNKS,
            tokens=tokens,
        )
        sums.append(got)
        return token

    below, above = [[] for _ in range(CHUNKS)], [[] for _ in range(CHUNKS)]

    def arrived(part, t):
        return [(part, blocks - 1 - t, below[part][t]), (part, 1 + t, above[part][t])]

    def pair_piece(part, t):
        return lambda source: pairs(([(part, 0, sent[part])] if t == 0 else []) + arrived(part, t), [source])

    fill = [weight_piece(part) for part in range(CHUNKS)]
    fill += [pair_piece(part, t) for t in range(blocks - 2) for part in range(CHUNKS)]
    token = chain_gathers(sent, blocks, below, above, fill)
    for run in fill:
        token = run(sent[-1])
    pairs(sum([arrived(part, blocks - 2) for part in range(CHUNKS)], []), [ordered] + ([] if token is None else [token]))
    spectral_grad = gradient[0]
    lift_own = jnp.sum(sum(sums), axis=(2, 3)).T
    lift_local = jnp.sum(sum(local_sums), axis=(2, 3)).T
    lift_own = jnp.concatenate([lift_own + lift_local[:, :chans], lift_local[:, chans:]], 1) * norm_scale
    packed = all_sum(jnp.concatenate([ordered.reshape(-1), lift_own.reshape(-1)]), ("dp", "blk"))
    local_grad = packed[: ordered.size].reshape(ordered.shape)
    lift_own = packed[ordered.size :].reshape(lift_own.shape)
    theirs = swap_cores(lift_own)
    mine = lift_own[:, :chans] + theirs[:, chans:]
    his = lift_own[:, chans:] + theirs[:, :chans]
    lift_grad = jnp.where(core == 0, jnp.concatenate([mine, his], 1), jnp.concatenate([his, mine], 1))
    return (spectral_grad, local_grad, lift_grad)


def solution(mesh):
    in_specs = (
        P("dp", "parts", "blk", None),
        P("parts", None),
        P("parts", "chan"),
        P("parts", ("blk", "dp"), "chan", None, None),
        P("dp", "chan", "blk", "parts"),
    )
    out_specs = (
        P("parts", ("blk", "dp"), "chan", None, None),
        P("parts", "chan"),
        P("parts", None),
    )
    return jax.shard_map(per_device, mesh=mesh, in_specs=in_specs, out_specs=out_specs, check_vma=False)
```

```python
import functools
import math

import jax
import jax.numpy as jnp
import ml_dtypes
import numpy as np
from jax import lax
from jax.experimental import pallas as pl
from jax.experimental.pallas import tpu as pltpu
from jax.sharding import PartitionSpec as P

BF = jnp.bfloat16
F32 = jnp.float32
TWO_PI = 2.0 * math.pi
CHUNKS = 2
VMEM = 48 * 1024 * 1024


def table(freqs, points, length):
    product = (freqs % length)[:, None] * points[None, :] % length
    angle = np.float32(TWO_PI / length) * product.astype(np.float32)
    return np.cos(angle), np.sin(angle)


def column_table(cells, modes):
    cos, sin = table(np.arange(modes), np.arange(cells), cells)
    return np.ascontiguousarray(np.concatenate([cos, -sin], 0).T).astype(ml_dtypes.bfloat16)


def row_tables(rows, modes, blocks, samples):
    index = np.arange(modes)
    cos, sin = table(np.where(index < modes // 2, index, index - modes), np.arange(rows), rows)
    both = np.stack([cos, sin]).astype(ml_dtypes.bfloat16)
    sub = modes // (blocks * samples)
    piece = sub // CHUNKS
    local = rows // blocks
    out = np.empty((blocks, samples, 2 * modes, local), ml_dtypes.bfloat16)
    for z in range(blocks):
        part = both[:, :, z * local : (z + 1) * local]
        for s in range(samples):
            order = np.concatenate(
                [
                    np.arange(piece) + piece * c + sub * ((s ^ j) + samples * ((z + d) % blocks))
                    for d in range(blocks)
                    for c in range(CHUNKS)
                    for j in range(samples)
                ]
            )
            out[z, s] = part[:, order].reshape(2 * modes, local)
    return out


def gelu_slope(value):
    return 0.5 * (1.0 + lax.erf(value * (1.0 / math.sqrt(2.0)))) + value * jnp.exp(-0.5 * value * value) * (
        1.0 / math.sqrt(2.0 * math.pi)
    )


def lift_rows(fields, lw, chan):
    total = fields[0] * lw[0, chan]
    for j in range(1, len(fields)):
        total = total + fields[j] * lw[j, chan]
    return jnp.tanh(total)


def row_forward(u, row_tab, scale):
    modes, width = row_tab.shape[0] // 2, u.shape[1] // 2
    prod = jnp.dot(row_tab, u, preferred_element_type=F32)
    real = (prod[:modes, :width] + prod[modes:, width:]) * scale
    imag = (prod[:modes, width:] - prod[modes:, :width]) * scale
    return jnp.concatenate([real.astype(BF), imag.astype(BF)], 1)


def split_modes(value, outs, at):
    rows = outs[0][0].shape[1]
    for c, part in enumerate(outs):
        for d, out in enumerate(part):
            lo = (d * len(outs) + c) * rows
            out[at] = value[lo : lo + rows]


def by_part(refs):
    each = len(refs) // CHUNKS
    return [refs[i * each : (i + 1) * each] for i in range(CHUNKS)]


def lift_kernel(bunch, scale, lw, fields, col, row_tab, lifted, *outs):
    group, rows, cells = lifted.shape
    first = pl.program_id(0) * group
    lanes = min(cells, 512)
    for b in range(0, group, bunch):
        for lo in range(0, rows, 16):
            for at in range(0, cells, lanes):
                f = [fields[j, lo : lo + 16, at : at + lanes].astype(F32) for j in range(fields.shape[0])]
                for c in range(b, b + bunch):
                    lifted[c, lo : lo + 16, at : at + lanes] = lift_rows(f, lw, first + c).astype(BF)
        u = jnp.dot(lifted[b : b + bunch].reshape(bunch * rows, cells), col[...], preferred_element_type=F32).astype(BF)
        for c in range(bunch):
            split_modes(row_forward(u[c * rows : (c + 1) * rows], row_tab[...], scale), by_part(outs), b + c)


def slope_kernel(scale, first, lw, fields, col, row_tab, *refs):
    out, token = refs[-2:]
    inputs, rows, cells = fields.shape
    blocks, group, sub = out.shape[0], out.shape[1], out.shape[3]
    for c in range(group):
        chan = first + pl.program_id(0) * group + c
        w = [[] for _ in range(inputs)]
        for lo in range(0, rows, 16):
            f = [fields[j, lo : lo + 16].astype(F32) for j in range(inputs)]
            t = lift_rows(f, lw, chan)
            slope = 1.0 - t * t
            for j in range(inputs):
                w[j].append((f[j] * slope).astype(BF))
        u = jnp.dot(jnp.concatenate(sum(w, []), 0), col[...], preferred_element_type=F32).astype(BF)
        for j in range(inputs):
            v = row_forward(u[j * rows : (j + 1) * rows], row_tab[...], scale)
            for d in range(blocks):
                out[d, c, j] = v[d * sub : (d + 1) * sub]
    token[...] = jnp.zeros(token.shape, F32)


def pair_kernel(n, *refs):
    out, token = refs[-2:]
    for c in range(out.shape[0]):
        back = [b[c].astype(F32) for b in refs[:n]]
        for j in range(out.shape[1]):
            total = None
            for b, f in zip(back, refs[n : 2 * n], strict=True):
                for r in range(0, b.shape[0], 8):
                    prod = b[r : r + 8] * f[0, c, j, r : r + 8].astype(F32)
                    total = prod if total is None else total + prod
            tile = total[:, :128]
            for k in range(128, total.shape[1], 128):
                tile = tile + total[:, k : k + 128]
            out[c, j] = tile
    token[...] = jnp.zeros(token.shape, F32)


def local_kernel(mix, own, other, out, token):
    n, rows, cells = own.shape
    for lo in range(0, cells, 256):
        at = pl.ds(lo, 256)
        both = jnp.concatenate([own[:, :, at].reshape(n * rows, 256), other[:, :, at].reshape(n * rows, 256)], 0)
        got = jnp.dot(mix[...], both, preferred_element_type=F32)
        out[:, :, at] = got.reshape(-1, rows, 256)
    token[...] = jnp.zeros(token.shape, F32)


def local_back_kernel(lw, mix, fields, own, other, grad, terms, sums):
    n, rows, cells = own.shape
    inputs = fields.shape[0]

    @pl.when(pl.program_id(0) == 0)
    def _():
        terms[...] = jnp.zeros(terms.shape, F32)
        sums[...] = jnp.zeros(sums.shape, F32)

    g = grad[...].reshape(-1, cells)
    for half, part in enumerate((own, other)):
        terms[half] += lax.dot_general(
            part[...].reshape(n * rows, cells), g, (((1,), (1,)), ((), ())), preferred_element_type=F32
        )

    def lanes(step, _):
        at = pl.ds(pl.multiple_of(step * 256, 256), 256)
        back = jnp.dot(mix[...], grad[:, :, at].reshape(-1, 256), preferred_element_type=F32)
        f = [fields[j, :, at].astype(F32) for j in range(inputs)]
        for c in range(2 * n):
            t = lift_rows(f, lw, c)
            total = back[c * rows : (c + 1) * rows] * (1.0 - t * t)
            for j in range(inputs):
                prod = f[j] * total
                prod = prod[:, :128] + prod[:, 128:]
                tile = prod[:8]
                for r in range(8, rows, 8):
                    tile = tile + prod[r : r + 8]
                sums[c, j] += tile
        return 0

    lax.fori_loop(0, cells // 256, lanes, 0)


def row_inverse(refs, chan, row_inv):
    rows = row_inv.shape[0] // 2
    width = refs[0].shape[-1] // 2
    hops = (len(refs) - 1) // 2
    blocks = [refs[0][chan]]
    for s in range(hops - 1, -1, -1):
        blocks.append(refs[1 + s][chan] + refs[hops + hops - s][chan])
    prod = jnp.dot(row_inv, jnp.concatenate(blocks, 0), preferred_element_type=F32)
    real = prod[:rows, :width] - prod[rows:, width:]
    imag = prod[:rows, width:] + prod[rows:, :width]
    return jnp.concatenate([real.astype(BF), imag.astype(BF)], 1)


def middle_kernel(blocks, bunch, grid_scale, scale, local, cotan, col, col_inv, row_tab, row_inv, *refs):
    n_in = 2 * blocks - 1
    grad, outs = refs[n_in], refs[n_in + 1 :]
    group, rows, cells = grad.shape
    for b in range(0, group, bunch):
        h = jnp.concatenate([row_inverse(refs[:n_in], c, row_inv[...]) for c in range(b, b + bunch)], 0)
        grid = jnp.dot(h, col_inv[...], preferred_element_type=F32)
        for c in range(bunch):
            for lo in range(0, rows, 16):
                pre = grid[c * rows + lo : c * rows + lo + 16] * grid_scale + local[b + c, lo : lo + 16]
                slope = cotan[0, b + c, lo : lo + 16].astype(F32) * gelu_slope(pre)
                grad[b + c, lo : lo + 16] = slope.astype(BF)
        u = jnp.dot(grad[b : b + bunch].reshape(bunch * rows, cells), col[...], preferred_element_type=F32).astype(BF)
        for c in range(bunch):
            split_modes(row_forward(u[c * rows : (c + 1) * rows], row_tab[...], scale), by_part(outs), b + c)


def mix_kernel(samples, core, w_keep, w_send, *refs):
    xs, keep, send = refs[:samples], refs[samples], refs[samples + 1]
    width = w_keep.shape[-1]
    ins, outs = w_keep.shape[2], w_keep.shape[3]
    for lo in range(0, width, 128):
        re, im = pl.ds(lo, 128), pl.ds(width + lo, 128)
        xr = [x[0, :, re].astype(F32) for x in xs]
        xi = [x[0, :, im].astype(F32) for x in xs]
        for w, out in ((w_keep, keep), (w_send, send)):
            real = [jnp.zeros((outs, 128), F32) for _ in range(samples)]
            imag = [jnp.zeros((outs, 128), F32) for _ in range(samples)]
            for i in range(ins):
                wr = w[0, 0, i, :, re].astype(F32)
                wi = w[1, 0, i, :, re].astype(F32)
                for s in range(samples):
                    a, b = xr[s][i : i + 1], xi[s][i : i + 1]
                    real[s] = real[s] + (wr * a - wi * b)
                    imag[s] = imag[s] + (wr * b + wi * a)
            for s in range(samples):
                out[s, 0, :, re] = real[s].astype(BF)
                out[s, 0, :, im] = imag[s].astype(BF)


def back_kernel(samples, core, w_own, w_other, g_other, *refs):
    gs, out = refs[:samples], refs[samples]
    width = w_own.shape[-1]
    ins, outs = w_own.shape[2], w_own.shape[3]
    for lo in range(0, width, 128):
        re, im = pl.ds(lo, 128), pl.ds(width + lo, 128)
        gr = [[g[0, :, re].astype(F32) for g in gs], [g_other[s, 0, :, re].astype(F32) for s in range(samples)]]
        gi = [[g[0, :, im].astype(F32) for g in gs], [g_other[s, 0, :, im].astype(F32) for s in range(samples)]]
        real = [[] for _ in range(samples)]
        imag = [[] for _ in range(samples)]
        for i in range(ins):
            w = [
                (w_own[0, 0, i, :, re].astype(F32), w_own[1, 0, i, :, re].astype(F32)),
                (w_other[0, 0, i, :, re].astype(F32), w_other[1, 0, i, :, re].astype(F32)),
            ]
            for s in range(samples):
                r = m = None
                for half in range(2):
                    wr, wi = w[half]
                    a, b = gr[half][s], gi[half][s]
                    r1 = wr * a + wi * b
                    m1 = wr * b - wi * a
                    r, m = (r1, m1) if r is None else (r + r1, m + m1)
                real[s].append(jnp.sum(r, axis=0, keepdims=True))
                imag[s].append(jnp.sum(m, axis=0, keepdims=True))
        for s in range(samples):
            out[s, 0, :, re] = jnp.concatenate(real[s], 0).astype(BF)
            out[s, 0, :, im] = jnp.concatenate(imag[s], 0).astype(BF)


def weight_kernel(samples, core, *refs):
    g_other, out, token = refs[0], refs[-2], refs[-1]
    xs, gs = refs[1 : 1 + samples], refs[1 + samples : 1 + 2 * samples]
    ins, half = xs[0].shape[1], gs[0].shape[1]
    width = xs[0].shape[2] // 2
    own = pl.ds(pl.multiple_of(core[0] * half, half), half)
    other = pl.ds(pl.multiple_of((1 - core[0]) * half, half), half)
    for lo in range(0, width, 128):
        re, im = pl.ds(lo, 128), pl.ds(width + lo, 128)
        xr = [x[0, :, re].astype(F32) for x in xs]
        xi = [x[0, :, im].astype(F32) for x in xs]
        for where in (own, other):
            if where is own:
                gr = [g[0, :, re].astype(F32) for g in gs]
                gi = [g[0, :, im].astype(F32) for g in gs]
            else:
                gr = [g_other[s, 0, :, re].astype(F32) for s in range(samples)]
                gi = [g_other[s, 0, :, im].astype(F32) for s in range(samples)]
            for i in range(ins):
                real = imag = None
                for s in range(samples):
                    a, b = xr[s][i : i + 1], xi[s][i : i + 1]
                    r1 = gr[s] * a + gi[s] * b
                    m1 = gi[s] * a - gr[s] * b
                    real, imag = (r1, m1) if real is None else (real + r1, imag + m1)
                out[0, 0, i, where, re] = real.astype(BF)
                out[1, 0, i, where, re] = imag.astype(BF)
    token[...] = jnp.zeros(token.shape, F32)


TOKEN = ((8, 128), F32, (8, 128), lambda i, *_: (0, 0))


def call(body, grid, ins, outs, flops, transcendentals=0, prefetch=None, tokens=(), into=None, vmem=VMEM):
    scalars = 0 if prefetch is None else 1

    def spec(block, index):
        if block is None:
            return pl.BlockSpec(memory_space=pltpu.SMEM)
        return pl.BlockSpec(block, index)

    moved = 0
    for a, block, _ in ins:
        moved += a.size * a.dtype.itemsize if block is None else math.prod(n for n in block if isinstance(n, int)) * math.prod(grid) * a.dtype.itemsize
    moved += sum(math.prod(b) * math.prod(grid) * jnp.dtype(t).itemsize for _, t, b, _ in outs)
    extra = list(tokens) + ([] if into is None else [into])

    def kernel(*refs):
        n = scalars + len(ins)
        body(*refs[:n], *refs[n + len(extra) :])

    return pl.pallas_call(
        kernel,
        grid_spec=pltpu.PrefetchScalarGridSpec(
            num_scalar_prefetch=scalars,
            grid=grid,
            in_specs=[spec(b, i) for _, b, i in ins] + [pl.BlockSpec(memory_space=pl.ANY)] * len(extra),
            out_specs=[spec(b, i) for _, _, b, i in outs],
        ),
        out_shape=[jax.ShapeDtypeStruct(s, t) for s, t, _, _ in outs],
        input_output_aliases={} if into is None else {scalars + len(ins) + len(extra) - 1: 0},
        compiler_params=pltpu.CompilerParams(vmem_limit_bytes=vmem),
        cost_estimate=pl.CostEstimate(flops=int(flops), bytes_accessed=int(moved), transcendentals=int(transcendentals)),
    )(*(() if prefetch is None else (prefetch,)), *[a for a, _, _ in ins], *extra)


def hold(value, *tokens):
    if not tokens:
        return value
    tokens = list(tokens)
    anywhere = pl.BlockSpec(memory_space=pl.ANY)
    return pl.pallas_call(
        lambda *refs: None,
        in_specs=[anywhere] * (1 + len(tokens)),
        out_specs=anywhere,
        out_shape=jax.ShapeDtypeStruct(value.shape, value.dtype),
        input_output_aliases={0: 0},
        cost_estimate=pl.CostEstimate(flops=0, bytes_accessed=0, transcendentals=0),
    )(value, *tokens)


def add_kernel(a, b, c, d, up, down):
    up[...] = (a[...].astype(F32) + b[...].astype(F32)).astype(BF)
    down[...] = (c[...].astype(F32) + d[...].astype(F32)).astype(BF)


def add_pairs(a, b, c, d, tokens):
    n = a.shape[0] // 2
    part = ((n, *a.shape[1:]), lambda i, *_: (i, 0, 0))
    return call(
        add_kernel, (2,), [(v, *part) for v in (a, b, c, d)], [(a.shape, BF, *part)] * 2, 4 * a.size, tokens=tokens
    )


def spaced(fill):
    return [run for f in fill for run in [f] + [None] * (CHUNKS - 1)]


def run_next(fill, source):
    run = fill.pop(0) if fill else None
    got = [] if run is None else run(source)
    return got if isinstance(got, list) else [got]


def chain_sums(shares, fill):
    hops = len(shares[0]) - 1
    blocks = hops + 1
    got = [None] * len(shares)
    tokens = []
    for t in range(hops):
        for p, part in enumerate(shares):
            up, down = part[hops - t], part[t + 1]
            if t:
                up, down = add_pairs(up, got[p][1], down, got[p][2], tokens)
            else:
                up, down = hold(up, *tokens), hold(down, *tokens)
            below = lax.ppermute(up, "blk", [(z, z + 1) for z in range(t + 1)])
            above = lax.ppermute(down, "blk", [(blocks - 1 - z, blocks - 2 - z) for z in range(t + 1)])
            got[p] = (part[0], below, above)
            tokens = run_next(fill, up)
    return got


def chain_gather(own, blocks, below, above, fill):
    tokens = []
    for t in range(blocks - 1):
        if tokens:
            below[-1], above[-1] = hold(below[-1], *tokens), hold(above[-1], *tokens)
        up, down = (below[-1], above[-1]) if t else (own, own)
        below.append(lax.ppermute(up, "blk", [(z, z + 1) for z in range(t, blocks - 1)]))
        above.append(lax.ppermute(down, "blk", [(blocks - 1 - z, blocks - 2 - z) for z in range(t, blocks - 1)]))
        tokens = run_next(fill, up)
    return tokens


def swap_samples(pieces):
    n = len(pieces)
    return [pieces[0]] + [lax.ppermute(pieces[j], "dp", [(i, i ^ j) for i in range(n)]) for j in range(1, n)]


def swap_cores(value):
    return lax.ppermute(value, "chan", [(0, 1), (1, 0)])


def to_modes(parts, samples):
    got = []
    for own, below, above in parts:
        total = (own.astype(F32) + below.astype(F32) + above.astype(F32)).astype(BF).transpose(1, 0, 2)
        sub = total.shape[0] // samples
        got.append((total, swap_samples([total[j * sub : (j + 1) * sub] for j in range(samples)])))
    return got


def from_modes(parts):
    return jnp.concatenate([a for pieces in parts for a in pieces], 0).transpose(1, 0, 2)


def all_sum(value, axes):
    for axis in axes:
        n = lax.axis_size(axis)
        values = [value] + [lax.ppermute(value, axis, [(i, i ^ j) for i in range(n)]) for j in range(1, n)]
        while len(values) > 1:
            values = [a + b for a, b in zip(values[::2], values[1::2], strict=True)]
        value = values[0]
    return value


def per_device(fields, lift_weight, local_weight, spectral_weight, cotangent):
    blocks = lax.axis_size("blk")
    samples = lax.axis_size("dp")
    sample = fields[0]
    inputs, rows, cells = sample.shape
    chans = cotangent.shape[1]
    mode_dev = spectral_weight.shape[1]
    half = spectral_weight.shape[3] // 2
    freqs = spectral_weight.shape[4]
    width = 2 * freqs
    modes = mode_dev * blocks * samples
    sub = modes // blocks
    piece = mode_dev // CHUNKS
    all_rows = rows * blocks
    z, s, core = lax.axis_index("blk"), lax.axis_index("dp"), lax.axis_index("chan")
    core_ref = core.astype(jnp.int32)[None]
    unit_scale = 1.0 / math.sqrt(all_rows * cells)
    norm_scale = 1.0 / math.sqrt(samples * all_rows * cells)

    col = jnp.asarray(column_table(cells, freqs))
    col_inv = jnp.asarray(np.ascontiguousarray(column_table(cells, freqs).T))
    row_all = jnp.asarray(row_tables(all_rows, modes, blocks, samples))
    row_tab = lax.dynamic_slice(row_all, (z, s, 0, 0), (1, 1, 2 * modes, rows))[0, 0]
    row_inv = row_tab.reshape(2, modes, rows).transpose(0, 2, 1).reshape(2 * rows, modes)
    lw_wide = lift_weight.astype(F32)
    own_lw = lax.dynamic_slice_in_dim(lw_wide, core * chans, chans, 1)
    both_lw = jnp.concatenate([own_lw, lax.dynamic_slice_in_dim(lw_wide, (1 - core) * chans, chans, 1)], 1)
    lw_rows = jnp.concatenate(
        [
            lax.dynamic_slice_in_dim(local_weight, core * chans, chans, 0),
            lax.dynamic_slice_in_dim(local_weight, (1 - core) * chans, chans, 0),
        ],
        0,
    )
    group_rows = 16
    eye = jnp.eye(group_rows, dtype=BF)
    spread = (lw_rows[:, None, :, None] * eye[None, :, None, :]).reshape(2 * chans * group_rows, chans * group_rows)

    def whole(a):
        return (a, a.shape, lambda i, *_: (0,) * a.ndim)

    def channel(a, n=1):
        return (a, (n, *a.shape[1:]), lambda i, *_: (i,) + (0,) * (a.ndim - 1))

    def part_outs(n):
        shape = (chans, sub // CHUNKS, width)
        return [(shape, BF, (n, *shape[1:]), lambda i, *_: (i, 0, 0)) for _ in range(CHUNKS * blocks)]

    matrix = chans * rows * 4 * freqs * (cells + 2 * modes)
    group, bunch = math.gcd(chans, 8), math.gcd(chans, 4)
    lifted, *shares = call(
        lambda place, *refs: lift_kernel(bunch, unit_scale, *refs),
        (chans // group,),
        [
            (own_lw, None, None),
            whole(sample),
            whole(col),
            (row_all, (pl.squeezed, pl.squeezed, 2 * modes, rows), lambda i, place: (place[0], place[1], 0, 0)),
        ],
        [((chans, rows, cells), BF, (group, rows, cells), lambda i, *_: (i, 0, 0)), *part_outs(group)],
        matrix,
        chans * rows * cells,
        prefetch=jnp.stack([z, s]).astype(jnp.int32),
    )
    shares = by_part(shares)
    lifted_other = swap_cores(lifted)

    slopes = [None]

    def slope_piece(first, count):
        def run(source):
            got, token = call(
                functools.partial(slope_kernel, unit_scale, first),
                (count // 2,),
                [(own_lw, None, None), whole(sample), whole(col), whole(row_tab)],
                [
                    (
                        (blocks, chans, inputs, sub, width),
                        BF,
                        (blocks, 2, inputs, sub, width),
                        lambda i, *_, first=first: (0, first // 2 + i, 0, 0, 0),
                    ),
                    TOKEN,
                ],
                matrix * inputs * count // chans,
                count * rows * cells,
                tokens=(source,),
                into=slopes[0],
            )
            slopes[0] = got
            return token

        return run

    locals_ = [None]

    def local_piece(first, count):
        def run(source):
            at = lambda i, *_: (0, first + i, 0)
            locals_[0], token = call(
                local_kernel,
                (count,),
                [
                    whole(spread.T),
                    (lifted, (chans, group_rows, cells), at),
                    (lifted_other, (chans, group_rows, cells), at),
                ],
                [((chans, rows, cells), F32, (chans, group_rows, cells), at), TOKEN],
                4 * chans * chans * group_rows * group_rows * count * cells,
                tokens=(source,),
                into=locals_[0],
            )
            return token

        return run

    def weight_half(part, other):
        return (
            spectral_weight,
            (2, 1, chans, half, freqs),
            lambda i, c, part=part, other=other: (0, part * piece + i, 0, (1 - c[0]) if other else c[0], 0),
        )

    def row_mode(a):
        return (a, (1, *a.shape[1:]), lambda i, *_: (i, 0, 0))

    def stacked(a):
        return (a, (samples, 1, *a.shape[2:]), lambda i, *_: (0, i, 0, 0))

    def stack_out(n):
        return ((samples, piece, n, width), BF, (samples, 1, n, width), lambda i, *_: (0, i, 0, 0))

    mix_flops = 16 * samples * piece * chans * half * freqs
    count = math.gcd(chans, 4)
    slope_fill = [slope_piece(i, count) for i in range(0, chans, count)]
    field_modes = []

    arrivals = to_modes(chain_sums(shares, spaced(slope_fill[:-1])), samples)
    parts = []
    for part in range(CHUNKS):
        xs = arrivals[part][1]
        field_modes.append(xs)
        keep, send = call(
            functools.partial(mix_kernel, samples),
            (piece,),
            [weight_half(part, False), weight_half(part, True), *[row_mode(x) for x in xs]],
            [stack_out(half)] * 2,
            mix_flops,
            prefetch=core_ref,
            tokens=[total for total, _ in arrivals[part + 1 :]],
        )
        send = hold(send, *[x for _, later in arrivals[part + 1 :] for x in later[1:]])
        total = (keep.astype(F32) + swap_cores(send).astype(F32)).astype(BF)
        parts.append(swap_samples([total[j] for j in range(samples)]))
    out_modes = from_modes(parts)
    steps = rows // group_rows
    count = -(-steps // 2)
    fill = [local_piece(i, min(count, steps - i)) for i in range(0, steps, count)]
    below, above = [], []
    chain_gather(out_modes, blocks, below, above, fill)
    for run in fill:
        run(out_modes)
    local = locals_[0]

    grad_z, *shares = call(
        functools.partial(middle_kernel, blocks, math.gcd(chans, 2), 2.0 * unit_scale, 2.0 * unit_scale),
        (chans // bunch,),
        [
            channel(local, bunch),
            (cotangent, (1, bunch, rows, cells), lambda i, *_: (0, i, 0, 0)),
            whole(col),
            whole(col_inv),
            whole(row_tab),
            whole(row_inv),
            *[channel(a, bunch) for a in (out_modes, *below, *above)],
        ],
        [((chans, rows, cells), BF, (bunch, rows, cells), lambda i, *_: (i, 0, 0)), *part_outs(bunch)],
        2 * matrix,
        3 * chans * rows * cells,
        vmem=60 * 1024 * 1024,
    )
    shares = by_part(shares)

    terms, local_sums = [], []

    def back_piece(first, count):
        at = lambda i, *_: (0, first + i, 0)

        def run(source):
            t, v = call(
                local_back_kernel,
                (count,),
                [
                    (both_lw, None, None),
                    whole(spread),
                    (sample, (inputs, group_rows, cells), at),
                    (lifted, (chans, group_rows, cells), at),
                    (lifted_other, (chans, group_rows, cells), at),
                    (grad_z, (chans, group_rows, cells), at),
                ],
                [
                    (
                        (2, chans * group_rows, chans * group_rows),
                        F32,
                        (2, chans * group_rows, chans * group_rows),
                        lambda i, *_: (0, 0, 0),
                    ),
                    ((2 * chans, inputs, 8, 128), F32, (2 * chans, inputs, 8, 128), lambda i, *_: (0, 0, 0, 0)),
                ],
                8 * chans * chans * group_rows * group_rows * count * cells,
                2 * chans * group_rows * count * cells,
                tokens=(source,),
            )
            terms.append(t)
            local_sums.append(v)
            return v

        return run

    steps = rows // group_rows
    count = -(-steps // 4)
    back_fill = [back_piece(i, min(count, steps - i)) for i in range(0, steps, count)]
    grad_modes, grad_others = [], []

    arrivals = to_modes(chain_sums(shares, spaced(back_fill[:-1])), samples)
    parts = []
    for part in range(CHUNKS):
        gs = arrivals[part][1]
        other = swap_cores(jnp.stack(gs))
        grad_modes.append(gs)
        grad_others.append(other)
        (back,) = call(
            functools.partial(back_kernel, samples),
            (piece,),
            [weight_half(part, False), weight_half(part, True), stacked(other), *[row_mode(g) for g in gs]],
            [stack_out(chans)],
            mix_flops,
            prefetch=core_ref,
            tokens=[total for total, _ in arrivals[part + 1 :]],
        )
        parts.append(swap_samples([back[j] for j in range(samples)]))
    back_modes = from_modes(parts)
    below, above = [], []

    gradient = [None]

    def weight_piece(part):
        def run(source):
            gradient[0], token = call(
                functools.partial(weight_kernel, samples),
                (piece,),
                [
                    stacked(grad_others[part]),
                    *[row_mode(x) for x in field_modes[part]],
                    *[row_mode(g) for g in grad_modes[part]],
                ],
                [
                    (
                        (2, mode_dev, chans, 2 * half, freqs),
                        BF,
                        (2, 1, chans, 2 * half, freqs),
                        lambda i, *_: (0, part * piece + i, 0, 0, 0),
                    ),
                    TOKEN,
                ],
                mix_flops,
                prefetch=core_ref,
                tokens=(source,),
                into=gradient[0],
            )
            return token

        return run

    sums = []
    at_once = 4

    def pairs(modes_of, tokens=()):
        def spectra(d):
            return (slopes[0], (1, at_once, inputs, sub, width), lambda i, *_: (d, i, 0, 0, 0))

        got, token = call(
            functools.partial(pair_kernel, len(modes_of)),
            (chans // at_once,),
            [channel(a, at_once) for _, a in modes_of] + [spectra(d) for d, _ in modes_of],
            [((chans, inputs, 8, 128), F32, (at_once, inputs, 8, 128), lambda i, *_: (i, 0, 0, 0)), TOKEN],
            4 * len(modes_of) * chans * inputs * sub * width,
            tokens=tokens,
        )
        sums.append(got)
        return token

    def arrived(t):
        return [(blocks - 1 - t, below[t]), (1 + t, above[t])]

    def pair_piece(t):
        return lambda source: pairs(([(0, back_modes)] if t == 0 else []) + arrived(t), [source])

    def together(*runs):
        def run(source):
            return [r(source) for r in runs]

        return run

    fill = [
        together(*[weight_piece(part) for part in range(CHUNKS)], *slope_fill[-1:]),
        together(*back_fill[-1:], pair_piece(0)),
    ]
    fill += [pair_piece(t) for t in range(1, blocks - 2)]
    tokens = chain_gather(back_modes, blocks, below, above, fill)
    while fill:
        tokens = tokens + run_next(fill, back_modes)
    term = sum(terms).reshape(2 * chans, group_rows, chans, group_rows)
    term = jnp.sum(term * jnp.eye(group_rows, dtype=F32)[None, :, None, :], axis=(1, 3))
    own_first = jnp.stack([term[:chans], term[chans:]])
    ordered = jnp.where(core == 0, own_first, own_first[::-1]).reshape(2 * chans, chans)
    ordered = ordered * norm_scale

    pairs(arrived(blocks - 2), [ordered, *tokens])
    spectral_grad = gradient[0]
    lift_own = jnp.sum(sum(sums), axis=(2, 3)).T
    lift_local = jnp.sum(sum(local_sums), axis=(2, 3)).T
    lift_own = jnp.concatenate([lift_own + lift_local[:, :chans], lift_local[:, chans:]], 1) * norm_scale
    packed = all_sum(jnp.concatenate([ordered.reshape(-1), lift_own.reshape(-1)]), ("dp", "blk"))
    local_grad = packed[: ordered.size].reshape(ordered.shape)
    lift_own = packed[ordered.size :].reshape(lift_own.shape)
    theirs = swap_cores(lift_own)
    mine = lift_own[:, :chans] + theirs[:, chans:]
    his = lift_own[:, chans:] + theirs[:, :chans]
    lift_grad = jnp.where(core == 0, jnp.concatenate([mine, his], 1), jnp.concatenate([his, mine], 1))
    return (spectral_grad, local_grad, lift_grad)


def solution(mesh):
    in_specs = (
        P("dp", "parts", "blk", None),
        P("parts", None),
        P("parts", "chan"),
        P("parts", ("blk", "dp"), "chan", None, None),
        P("dp", "chan", "blk", "parts"),
    )
    out_specs = (
        P("parts", ("blk", "dp"), "chan", None, None),
        P("parts", "chan"),
        P("parts", None),
    )
    return jax.shard_map(per_device, mesh=mesh, in_specs=in_specs, out_specs=out_specs, check_vma=False)
```

```python
import functools
import math

import jax
import jax.numpy as jnp
import ml_dtypes
import numpy as np
from jax import lax
from jax.experimental import pallas as pl
from jax.experimental.pallas import tpu as pltpu
from jax.sharding import PartitionSpec as P

BF = jnp.bfloat16
F32 = jnp.float32
TWO_PI = 2.0 * math.pi
CHUNKS = 2
VMEM = 48 * 1024 * 1024


def table(freqs, points, length):
    product = (freqs % length)[:, None] * points[None, :] % length
    angle = np.float32(TWO_PI / length) * product.astype(np.float32)
    return np.cos(angle), np.sin(angle)


def column_table(cells, modes):
    cos, sin = table(np.arange(modes), np.arange(cells), cells)
    return np.ascontiguousarray(np.concatenate([cos, -sin], 0).T).astype(ml_dtypes.bfloat16)


def row_tables(rows, modes, blocks, samples):
    index = np.arange(modes)
    cos, sin = table(np.where(index < modes // 2, index, index - modes), np.arange(rows), rows)
    both = np.stack([cos, sin]).astype(ml_dtypes.bfloat16)
    sub = modes // (blocks * samples)
    piece = sub // CHUNKS
    local = rows // blocks
    out = np.empty((blocks, samples, 2 * modes, local), ml_dtypes.bfloat16)
    for z in range(blocks):
        part = both[:, :, z * local : (z + 1) * local]
        for s in range(samples):
            order = np.concatenate(
                [
                    np.arange(piece) + piece * c + sub * ((s ^ j) + samples * ((z + d) % blocks))
                    for d in range(blocks)
                    for c in range(CHUNKS)
                    for j in range(samples)
                ]
            )
            out[z, s] = part[:, order].reshape(2 * modes, local)
    return out


def gelu_slope(value):
    return 0.5 * (1.0 + lax.erf(value * (1.0 / math.sqrt(2.0)))) + value * jnp.exp(-0.5 * value * value) * (
        1.0 / math.sqrt(2.0 * math.pi)
    )


def lift_rows(fields, lw, chan):
    total = fields[0] * lw[0, chan]
    for j in range(1, len(fields)):
        total = total + fields[j] * lw[j, chan]
    return jnp.tanh(total)


def row_forward(u, row_tab, scale):
    modes, width = row_tab.shape[0] // 2, u.shape[1] // 2
    prod = jnp.dot(row_tab, u, preferred_element_type=F32)
    real = (prod[:modes, :width] + prod[modes:, width:]) * scale
    imag = (prod[:modes, width:] - prod[modes:, :width]) * scale
    return jnp.concatenate([real.astype(BF), imag.astype(BF)], 1)


def split_modes(value, outs, at):
    rows = outs[0][0].shape[1]
    for c, part in enumerate(outs):
        for d, out in enumerate(part):
            lo = (d * len(outs) + c) * rows
            out[at] = value[lo : lo + rows]


def by_part(refs):
    each = len(refs) // CHUNKS
    return [refs[i * each : (i + 1) * each] for i in range(CHUNKS)]


def lift_kernel(bunch, scale, lw, fields, col, row_tab, lifted, *outs):
    group, rows, cells = lifted.shape
    first = pl.program_id(0) * group
    lanes = min(cells, 512)
    for b in range(0, group, bunch):
        for lo in range(0, rows, 16):
            for at in range(0, cells, lanes):
                f = [fields[j, lo : lo + 16, at : at + lanes].astype(F32) for j in range(fields.shape[0])]
                for c in range(b, b + bunch):
                    lifted[c, lo : lo + 16, at : at + lanes] = lift_rows(f, lw, first + c).astype(BF)
        u = jnp.dot(lifted[b : b + bunch].reshape(bunch * rows, cells), col[...], preferred_element_type=F32).astype(BF)
        for c in range(bunch):
            split_modes(row_forward(u[c * rows : (c + 1) * rows], row_tab[...], scale), by_part(outs), b + c)


def slope_kernel(scale, first, lw, fields, col, row_tab, *refs):
    out, token = refs[-2:]
    inputs, rows, cells = fields.shape
    blocks, group, sub = out.shape[0], out.shape[1], out.shape[3]
    for c in range(group):
        chan = first + pl.program_id(0) * group + c
        w = [[] for _ in range(inputs)]
        for lo in range(0, rows, 16):
            f = [fields[j, lo : lo + 16].astype(F32) for j in range(inputs)]
            t = lift_rows(f, lw, chan)
            slope = 1.0 - t * t
            for j in range(inputs):
                w[j].append((f[j] * slope).astype(BF))
        u = jnp.dot(jnp.concatenate(sum(w, []), 0), col[...], preferred_element_type=F32).astype(BF)
        for j in range(inputs):
            v = row_forward(u[j * rows : (j + 1) * rows], row_tab[...], scale)
            for d in range(blocks):
                out[d, c, j] = v[d * sub : (d + 1) * sub]
    token[...] = jnp.zeros(token.shape, F32)


def pair_kernel(n, *refs):
    out, token = refs[-2:]
    for c in range(out.shape[0]):
        back = [b[c].astype(F32) for b in refs[:n]]
        for j in range(out.shape[1]):
            total = None
            for b, f in zip(back, refs[n : 2 * n], strict=True):
                for r in range(0, b.shape[0], 8):
                    prod = b[r : r + 8] * f[0, c, j, r : r + 8].astype(F32)
                    total = prod if total is None else total + prod
            tile = total[:, :128]
            for k in range(128, total.shape[1], 128):
                tile = tile + total[:, k : k + 128]
            out[c, j] = tile
    token[...] = jnp.zeros(token.shape, F32)


def local_kernel(mix, own, other, out, token):
    n, rows, cells = own.shape
    for lo in range(0, cells, 256):
        at = pl.ds(lo, 256)
        both = jnp.concatenate([own[:, :, at].reshape(n * rows, 256), other[:, :, at].reshape(n * rows, 256)], 0)
        got = jnp.dot(mix[...], both, preferred_element_type=F32)
        out[:, :, at] = got.reshape(-1, rows, 256)
    token[...] = jnp.zeros(token.shape, F32)


def local_back_kernel(lw, mix, fields, own, other, grad, *refs):
    earlier, (terms, sums) = refs[:-2], refs[-2:]
    n, rows, cells = own.shape
    inputs = fields.shape[0]

    @pl.when(pl.program_id(0) == 0)
    def _():
        for i, total in enumerate((terms, sums)):
            total[...] = earlier[i][...] if earlier else jnp.zeros(total.shape, F32)

    g = grad[...].reshape(-1, cells)
    for half, part in enumerate((own, other)):
        terms[half] += lax.dot_general(
            part[...].reshape(n * rows, cells), g, (((1,), (1,)), ((), ())), preferred_element_type=F32
        )

    for lo in range(0, cells, 256):
        at = pl.ds(lo, 256)
        back = jnp.dot(mix[...], grad[:, :, at].reshape(-1, 256), preferred_element_type=F32)
        f = [fields[j, :, at].astype(F32) for j in range(inputs)]
        for c in range(2 * n):
            t = lift_rows(f, lw, c)
            total = back[c * rows : (c + 1) * rows] * (1.0 - t * t)
            for j in range(inputs):
                prod = f[j] * total
                prod = prod[:, :128] + prod[:, 128:]
                tile = prod[:8]
                for r in range(8, rows, 8):
                    tile = tile + prod[r : r + 8]
                sums[c, j] += tile


def row_inverse(refs, chan, row_inv):
    rows = row_inv.shape[0] // 2
    width = refs[0].shape[-1] // 2
    hops = (len(refs) - 1) // 2
    blocks = [refs[0][chan]]
    for s in range(hops - 1, -1, -1):
        blocks.append(refs[1 + s][chan] + refs[hops + hops - s][chan])
    prod = jnp.dot(row_inv, jnp.concatenate(blocks, 0), preferred_element_type=F32)
    real = prod[:rows, :width] - prod[rows:, width:]
    imag = prod[:rows, width:] + prod[rows:, :width]
    return jnp.concatenate([real.astype(BF), imag.astype(BF)], 1)


def middle_kernel(blocks, bunch, grid_scale, scale, local, cotan, col, col_inv, row_tab, row_inv, *refs):
    n_in = 2 * blocks - 1
    grad, outs = refs[n_in], refs[n_in + 1 :]
    group, rows, cells = grad.shape
    for b in range(0, group, bunch):
        h = jnp.concatenate([row_inverse(refs[:n_in], c, row_inv[...]) for c in range(b, b + bunch)], 0)
        grid = jnp.dot(h, col_inv[...], preferred_element_type=F32)
        for c in range(bunch):
            for lo in range(0, rows, 16):
                pre = grid[c * rows + lo : c * rows + lo + 16] * grid_scale + local[b + c, lo : lo + 16]
                slope = cotan[0, b + c, lo : lo + 16].astype(F32) * gelu_slope(pre)
                grad[b + c, lo : lo + 16] = slope.astype(BF)
        u = jnp.dot(grad[b : b + bunch].reshape(bunch * rows, cells), col[...], preferred_element_type=F32).astype(BF)
        for c in range(bunch):
            split_modes(row_forward(u[c * rows : (c + 1) * rows], row_tab[...], scale), by_part(outs), b + c)


def mix_kernel(samples, core, w_keep, w_send, *refs):
    xs, keep, send = refs[:samples], refs[samples], refs[samples + 1]
    width = w_keep.shape[-1]
    ins, outs = w_keep.shape[2], w_keep.shape[3]
    for lo in range(0, width, 128):
        re, im = pl.ds(lo, 128), pl.ds(width + lo, 128)
        xr = [x[0, :, re].astype(F32) for x in xs]
        xi = [x[0, :, im].astype(F32) for x in xs]
        for w, out in ((w_keep, keep), (w_send, send)):
            real = [jnp.zeros((outs, 128), F32) for _ in range(samples)]
            imag = [jnp.zeros((outs, 128), F32) for _ in range(samples)]
            for i in range(ins):
                wr = w[0, 0, i, :, re].astype(F32)
                wi = w[1, 0, i, :, re].astype(F32)
                for s in range(samples):
                    a, b = xr[s][i : i + 1], xi[s][i : i + 1]
                    real[s] = real[s] + (wr * a - wi * b)
                    imag[s] = imag[s] + (wr * b + wi * a)
            for s in range(samples):
                out[s, 0, :, re] = real[s].astype(BF)
                out[s, 0, :, im] = imag[s].astype(BF)


def back_kernel(samples, core, w_own, w_other, g_other, *refs):
    gs, out = refs[:samples], refs[samples]
    width = w_own.shape[-1]
    ins, outs = w_own.shape[2], w_own.shape[3]
    for lo in range(0, width, 128):
        re, im = pl.ds(lo, 128), pl.ds(width + lo, 128)
        gr = [[g[0, :, re].astype(F32) for g in gs], [g_other[s, 0, :, re].astype(F32) for s in range(samples)]]
        gi = [[g[0, :, im].astype(F32) for g in gs], [g_other[s, 0, :, im].astype(F32) for s in range(samples)]]
        real = [[] for _ in range(samples)]
        imag = [[] for _ in range(samples)]
        for i in range(ins):
            w = [
                (w_own[0, 0, i, :, re].astype(F32), w_own[1, 0, i, :, re].astype(F32)),
                (w_other[0, 0, i, :, re].astype(F32), w_other[1, 0, i, :, re].astype(F32)),
            ]
            for s in range(samples):
                r = m = None
                for half in range(2):
                    wr, wi = w[half]
                    a, b = gr[half][s], gi[half][s]
                    r1 = wr * a + wi * b
                    m1 = wr * b - wi * a
                    r, m = (r1, m1) if r is None else (r + r1, m + m1)
                real[s].append(jnp.sum(r, axis=0, keepdims=True))
                imag[s].append(jnp.sum(m, axis=0, keepdims=True))
        for s in range(samples):
            out[s, 0, :, re] = jnp.concatenate(real[s], 0).astype(BF)
            out[s, 0, :, im] = jnp.concatenate(imag[s], 0).astype(BF)


def weight_kernel(samples, core, *refs):
    g_other, out, token = refs[0], refs[-2], refs[-1]
    xs, gs = refs[1 : 1 + samples], refs[1 + samples : 1 + 2 * samples]
    ins, half = xs[0].shape[1], gs[0].shape[1]
    width = xs[0].shape[2] // 2
    own = pl.ds(pl.multiple_of(core[0] * half, half), half)
    other = pl.ds(pl.multiple_of((1 - core[0]) * half, half), half)
    for lo in range(0, width, 128):
        re, im = pl.ds(lo, 128), pl.ds(width + lo, 128)
        xr = [x[0, :, re].astype(F32) for x in xs]
        xi = [x[0, :, im].astype(F32) for x in xs]
        for where in (own, other):
            if where is own:
                gr = [g[0, :, re].astype(F32) for g in gs]
                gi = [g[0, :, im].astype(F32) for g in gs]
            else:
                gr = [g_other[s, 0, :, re].astype(F32) for s in range(samples)]
                gi = [g_other[s, 0, :, im].astype(F32) for s in range(samples)]
            for i in range(ins):
                real = imag = None
                for s in range(samples):
                    a, b = xr[s][i : i + 1], xi[s][i : i + 1]
                    r1 = gr[s] * a + gi[s] * b
                    m1 = gi[s] * a - gr[s] * b
                    real, imag = (r1, m1) if real is None else (real + r1, imag + m1)
                out[0, 0, i, where, re] = real.astype(BF)
                out[1, 0, i, where, re] = imag.astype(BF)
    token[...] = jnp.zeros(token.shape, F32)


TOKEN = ((8, 128), F32, (8, 128), lambda i, *_: (0, 0))


def call(body, grid, ins, outs, flops, transcendentals=0, prefetch=None, tokens=(), into=None, vmem=VMEM):
    scalars = 0 if prefetch is None else 1

    def spec(block, index):
        if block is None:
            return pl.BlockSpec(memory_space=pltpu.SMEM)
        return pl.BlockSpec(block, index)

    moved = 0
    for a, block, _ in ins:
        moved += a.size * a.dtype.itemsize if block is None else math.prod(n for n in block if isinstance(n, int)) * math.prod(grid) * a.dtype.itemsize
    moved += sum(math.prod(b) * math.prod(grid) * jnp.dtype(t).itemsize for _, t, b, _ in outs)
    extra = list(tokens) + ([] if into is None else [into])

    def kernel(*refs):
        n = scalars + len(ins)
        body(*refs[:n], *refs[n + len(extra) :])

    return pl.pallas_call(
        kernel,
        grid_spec=pltpu.PrefetchScalarGridSpec(
            num_scalar_prefetch=scalars,
            grid=grid,
            in_specs=[spec(b, i) for _, b, i in ins] + [pl.BlockSpec(memory_space=pl.ANY)] * len(extra),
            out_specs=[spec(b, i) for _, _, b, i in outs],
        ),
        out_shape=[jax.ShapeDtypeStruct(s, t) for s, t, _, _ in outs],
        input_output_aliases={} if into is None else {scalars + len(ins) + len(extra) - 1: 0},
        compiler_params=pltpu.CompilerParams(vmem_limit_bytes=vmem),
        cost_estimate=pl.CostEstimate(flops=int(flops), bytes_accessed=int(moved), transcendentals=int(transcendentals)),
    )(*(() if prefetch is None else (prefetch,)), *[a for a, _, _ in ins], *extra)


def hold(value, *tokens):
    if not tokens:
        return value
    tokens = list(tokens)
    anywhere = pl.BlockSpec(memory_space=pl.ANY)
    return pl.pallas_call(
        lambda *refs: None,
        in_specs=[anywhere] * (1 + len(tokens)),
        out_specs=anywhere,
        out_shape=jax.ShapeDtypeStruct(value.shape, value.dtype),
        input_output_aliases={0: 0},
        cost_estimate=pl.CostEstimate(flops=0, bytes_accessed=0, transcendentals=0),
    )(value, *tokens)


def add_kernel(a, b, c, d, up, down):
    up[...] = (a[...].astype(F32) + b[...].astype(F32)).astype(BF)
    down[...] = (c[...].astype(F32) + d[...].astype(F32)).astype(BF)


def add_pairs(a, b, c, d, tokens):
    n = a.shape[0] // 2
    part = ((n, *a.shape[1:]), lambda i, *_: (i, 0, 0))
    return call(
        add_kernel, (2,), [(v, *part) for v in (a, b, c, d)], [(a.shape, BF, *part)] * 2, 4 * a.size, tokens=tokens
    )


def spaced(fill):
    return [None, *fill]


def run_next(fill, source):
    run = fill.pop(0) if fill else None
    got = [] if run is None else run(source)
    return got if isinstance(got, list) else [got]


def chain_sums(shares, fill):
    hops = len(shares[0]) - 1
    blocks = hops + 1
    got = [None] * len(shares)
    tokens = []
    for t in range(hops):
        for p, part in enumerate(shares):
            up, down = part[hops - t], part[t + 1]
            if t:
                up, down = add_pairs(up, got[p][1], down, got[p][2], tokens)
                tokens = []
            below = lax.ppermute(up, "blk", [(z, z + 1) for z in range(t + 1)])
            above = lax.ppermute(down, "blk", [(blocks - 1 - z, blocks - 2 - z) for z in range(t + 1)])
            got[p] = (part[0], below, above)
            tokens = tokens + run_next(fill, up)
    return got


def chain_gather(own, blocks, below, above, fill):
    tokens = []
    for t in range(blocks - 1):
        if tokens:
            below[-1], above[-1] = hold(below[-1], *tokens), hold(above[-1], *tokens)
        up, down = (below[-1], above[-1]) if t else (own, own)
        below.append(lax.ppermute(up, "blk", [(z, z + 1) for z in range(t, blocks - 1)]))
        above.append(lax.ppermute(down, "blk", [(blocks - 1 - z, blocks - 2 - z) for z in range(t, blocks - 1)]))
        tokens = run_next(fill, up)
    return tokens


def swap_samples(pieces):
    n = len(pieces)
    return [pieces[0]] + [lax.ppermute(pieces[j], "dp", [(i, i ^ j) for i in range(n)]) for j in range(1, n)]


def swap_cores(value):
    return lax.ppermute(value, "chan", [(0, 1), (1, 0)])


def to_modes(parts, samples):
    got = []
    for own, below, above in parts:
        total = (own.astype(F32) + below.astype(F32) + above.astype(F32)).astype(BF).transpose(1, 0, 2)
        sub = total.shape[0] // samples
        got.append((total, swap_samples([total[j * sub : (j + 1) * sub] for j in range(samples)])))
    return got


def from_modes(parts):
    return jnp.concatenate([a for pieces in parts for a in pieces], 0).transpose(1, 0, 2)


def all_sum(value, axes):
    for axis in axes:
        n = lax.axis_size(axis)
        values = [value] + [lax.ppermute(value, axis, [(i, i ^ j) for i in range(n)]) for j in range(1, n)]
        while len(values) > 1:
            values = [a + b for a, b in zip(values[::2], values[1::2], strict=True)]
        value = values[0]
    return value


def per_device(fields, lift_weight, local_weight, spectral_weight, cotangent):
    blocks = lax.axis_size("blk")
    samples = lax.axis_size("dp")
    sample = fields[0]
    inputs, rows, cells = sample.shape
    chans = cotangent.shape[1]
    mode_dev = spectral_weight.shape[1]
    half = spectral_weight.shape[3] // 2
    freqs = spectral_weight.shape[4]
    width = 2 * freqs
    modes = mode_dev * blocks * samples
    sub = modes // blocks
    piece = mode_dev // CHUNKS
    all_rows = rows * blocks
    z, s, core = lax.axis_index("blk"), lax.axis_index("dp"), lax.axis_index("chan")
    core_ref = core.astype(jnp.int32)[None]
    unit_scale = 1.0 / math.sqrt(all_rows * cells)
    norm_scale = 1.0 / math.sqrt(samples * all_rows * cells)

    col = jnp.asarray(column_table(cells, freqs))
    col_inv = jnp.asarray(np.ascontiguousarray(column_table(cells, freqs).T))
    row_all = jnp.asarray(row_tables(all_rows, modes, blocks, samples))
    row_tab = lax.dynamic_slice(row_all, (z, s, 0, 0), (1, 1, 2 * modes, rows))[0, 0]
    row_inv = row_tab.reshape(2, modes, rows).transpose(0, 2, 1).reshape(2 * rows, modes)
    lw_wide = lift_weight.astype(F32)
    own_lw = lax.dynamic_slice_in_dim(lw_wide, core * chans, chans, 1)
    both_lw = jnp.concatenate([own_lw, lax.dynamic_slice_in_dim(lw_wide, (1 - core) * chans, chans, 1)], 1)
    lw_rows = jnp.concatenate(
        [
            lax.dynamic_slice_in_dim(local_weight, core * chans, chans, 0),
            lax.dynamic_slice_in_dim(local_weight, (1 - core) * chans, chans, 0),
        ],
        0,
    )
    group_rows = 16
    eye = jnp.eye(group_rows, dtype=BF)
    spread = (lw_rows[:, None, :, None] * eye[None, :, None, :]).reshape(2 * chans * group_rows, chans * group_rows)

    def whole(a):
        return (a, a.shape, lambda i, *_: (0,) * a.ndim)

    def channel(a, n=1):
        return (a, (n, *a.shape[1:]), lambda i, *_: (i,) + (0,) * (a.ndim - 1))

    def part_outs(n):
        shape = (chans, sub // CHUNKS, width)
        return [(shape, BF, (n, *shape[1:]), lambda i, *_: (i, 0, 0)) for _ in range(CHUNKS * blocks)]

    matrix = chans * rows * 4 * freqs * (cells + 2 * modes)
    group, bunch = math.gcd(chans, 8), math.gcd(chans, 4)
    lifted, *shares = call(
        lambda place, *refs: lift_kernel(bunch, unit_scale, *refs),
        (chans // group,),
        [
            (own_lw, None, None),
            whole(sample),
            whole(col),
            (row_all, (pl.squeezed, pl.squeezed, 2 * modes, rows), lambda i, place: (place[0], place[1], 0, 0)),
        ],
        [((chans, rows, cells), BF, (group, rows, cells), lambda i, *_: (i, 0, 0)), *part_outs(group)],
        matrix,
        chans * rows * cells,
        prefetch=jnp.stack([z, s]).astype(jnp.int32),
    )
    shares = by_part(shares)
    lifted_other = swap_cores(lifted)

    slopes = [None]

    def slope_piece(first, count):
        def run(source):
            got, token = call(
                functools.partial(slope_kernel, unit_scale, first),
                (count // 2,),
                [(own_lw, None, None), whole(sample), whole(col), whole(row_tab)],
                [
                    (
                        (blocks, chans, inputs, sub, width),
                        BF,
                        (blocks, 2, inputs, sub, width),
                        lambda i, *_, first=first: (0, first // 2 + i, 0, 0, 0),
                    ),
                    TOKEN,
                ],
                matrix * inputs * count // chans,
                count * rows * cells,
                tokens=(source,),
                into=slopes[0],
            )
            slopes[0] = got
            return token

        return run

    def together(*runs):
        def run(source):
            return [r(source) for r in runs]

        return run

    locals_ = [None]

    def local_piece(first, count):
        def run(source):
            at = lambda i, *_: (0, first + i, 0)
            locals_[0], token = call(
                local_kernel,
                (count,),
                [
                    whole(spread.T),
                    (lifted, (chans, group_rows, cells), at),
                    (lifted_other, (chans, group_rows, cells), at),
                ],
                [((chans, rows, cells), F32, (chans, group_rows, cells), at), TOKEN],
                4 * chans * chans * group_rows * group_rows * count * cells,
                tokens=(source,),
                into=locals_[0],
            )
            return token

        return run

    def weight_half(part, other):
        return (
            spectral_weight,
            (2, 1, chans, half, freqs),
            lambda i, c, part=part, other=other: (0, part * piece + i, 0, (1 - c[0]) if other else c[0], 0),
        )

    def row_mode(a):
        return (a, (1, *a.shape[1:]), lambda i, *_: (i, 0, 0))

    def stacked(a):
        return (a, (samples, 1, *a.shape[2:]), lambda i, *_: (0, i, 0, 0))

    def stack_out(n):
        return ((samples, piece, n, width), BF, (samples, 1, n, width), lambda i, *_: (0, i, 0, 0))

    mix_flops = 16 * samples * piece * chans * half * freqs
    count = math.gcd(chans, 2)
    slope_fill = [slope_piece(i, count) for i in range(0, chans, count)]
    turns = CHUNKS * (blocks - 1) - 2
    field_modes = []

    arrivals = to_modes(chain_sums(shares, spaced(slope_fill[:turns])), samples)
    parts = []
    for part in range(CHUNKS):
        xs = arrivals[part][1]
        field_modes.append(xs)
        keep, send = call(
            functools.partial(mix_kernel, samples),
            (piece,),
            [weight_half(part, False), weight_half(part, True), *[row_mode(x) for x in xs]],
            [stack_out(half)] * 2,
            mix_flops,
            prefetch=core_ref,
            tokens=[total for total, _ in arrivals[part + 1 :]],
        )
        send = hold(send, *[x for _, later in arrivals[part + 1 :] for x in later[1:]])
        total = (keep.astype(F32) + swap_cores(send).astype(F32)).astype(BF)
        parts.append(swap_samples([total[j] for j in range(samples)]))
    out_modes = from_modes(parts)
    steps = rows // group_rows
    count = -(-steps // 2)
    fill = [local_piece(i, min(count, steps - i)) for i in range(0, steps, count)]
    below, above = [], []
    later = slope_fill[turns:]
    fill = [together(a, *later[i : i + 1]) for i, a in enumerate(fill)]
    fill.append(together(*later[len(fill) : len(fill) + 1]))
    later = later[len(fill) :]
    tokens = chain_gather(out_modes, blocks, below, above, fill)
    while fill:
        tokens = tokens + run_next(fill, out_modes)
    local = locals_[0]

    grad_z, *shares = call(
        functools.partial(middle_kernel, blocks, math.gcd(chans, 2), 2.0 * unit_scale, 2.0 * unit_scale),
        (chans // bunch,),
        [
            channel(local, bunch),
            (cotangent, (1, bunch, rows, cells), lambda i, *_: (0, i, 0, 0)),
            whole(col),
            whole(col_inv),
            whole(row_tab),
            whole(row_inv),
            *[channel(a, bunch) for a in (out_modes, *below, *above)],
        ],
        [((chans, rows, cells), BF, (bunch, rows, cells), lambda i, *_: (i, 0, 0)), *part_outs(bunch)],
        2 * matrix,
        3 * chans * rows * cells,
        tokens=tokens,
        vmem=60 * 1024 * 1024,
    )
    shares = by_part(shares)

    terms, local_sums = [], []

    def back_piece(first, count):
        at = lambda i, *_: (0, first + i, 0)

        def run(source):
            t, v = call(
                local_back_kernel,
                (count,),
                [
                    (both_lw, None, None),
                    whole(spread),
                    (sample, (inputs, group_rows, cells), at),
                    (lifted, (chans, group_rows, cells), at),
                    (lifted_other, (chans, group_rows, cells), at),
                    (grad_z, (chans, group_rows, cells), at),
                    *[whole(a) for a in (*terms[-1:], *local_sums[-1:])],
                ],
                [
                    (
                        (2, chans * group_rows, chans * group_rows),
                        F32,
                        (2, chans * group_rows, chans * group_rows),
                        lambda i, *_: (0, 0, 0),
                    ),
                    ((2 * chans, inputs, 8, 128), F32, (2 * chans, inputs, 8, 128), lambda i, *_: (0, 0, 0, 0)),
                ],
                8 * chans * chans * group_rows * group_rows * count * cells,
                2 * chans * group_rows * count * cells,
                tokens=(source,),
            )
            terms.append(t)
            local_sums.append(v)
            return v

        return run

    steps = rows // group_rows
    count = -(-steps // 8)
    back_fill = [back_piece(i, min(count, steps - i)) for i in range(0, steps, count)]
    grad_modes, grad_others = [], []

    arrivals = to_modes(chain_sums(shares, spaced([together(*back_fill[:3]), *back_fill[3 : turns + 2]])), samples)
    parts = []
    for part in range(CHUNKS):
        gs = arrivals[part][1]
        other = swap_cores(jnp.stack(gs))
        grad_modes.append(gs)
        grad_others.append(other)
        (back,) = call(
            functools.partial(back_kernel, samples),
            (piece,),
            [weight_half(part, False), weight_half(part, True), stacked(other), *[row_mode(g) for g in gs]],
            [stack_out(chans)],
            mix_flops,
            prefetch=core_ref,
            tokens=[total for total, _ in arrivals[part + 1 :]],
        )
        parts.append(swap_samples([back[j] for j in range(samples)]))
    back_modes = from_modes(parts)
    below, above = [], []

    gradient = [None]

    def weight_piece(part):
        def run(source):
            gradient[0], token = call(
                functools.partial(weight_kernel, samples),
                (piece,),
                [
                    stacked(grad_others[part]),
                    *[row_mode(x) for x in field_modes[part]],
                    *[row_mode(g) for g in grad_modes[part]],
                ],
                [
                    (
                        (2, mode_dev, chans, 2 * half, freqs),
                        BF,
                        (2, 1, chans, 2 * half, freqs),
                        lambda i, *_: (0, part * piece + i, 0, 0, 0),
                    ),
                    TOKEN,
                ],
                mix_flops,
                prefetch=core_ref,
                tokens=(source,),
                into=gradient[0],
            )
            return token

        return run

    sums = []
    at_once = 4

    def pairs(modes_of, tokens=()):
        def spectra(d):
            return (slopes[0], (1, at_once, inputs, sub, width), lambda i, *_: (d, i, 0, 0, 0))

        got, token = call(
            functools.partial(pair_kernel, len(modes_of)),
            (chans // at_once,),
            [channel(a, at_once) for _, a in modes_of] + [spectra(d) for d, _ in modes_of],
            [((chans, inputs, 8, 128), F32, (at_once, inputs, 8, 128), lambda i, *_: (i, 0, 0, 0)), TOKEN],
            4 * len(modes_of) * chans * inputs * sub * width,
            tokens=tokens,
        )
        sums.append(got)
        return token

    def arrived(t):
        return [(blocks - 1 - t, below[t]), (1 + t, above[t])]

    def pair_piece(t):
        return lambda source: pairs(([(0, back_modes)] if t == 0 else []) + arrived(t), [source])

    fill = [
        together(*[weight_piece(part) for part in range(CHUNKS)], *later),
        together(*back_fill[turns + 2 :]),
        together(*[pair_piece(t) for t in range(min(2, blocks - 2))]),
    ]
    fill += [pair_piece(t) for t in range(2, blocks - 2)]
    tokens = chain_gather(back_modes, blocks, below, above, fill)
    while fill:
        tokens = tokens + run_next(fill, back_modes)
    term = terms[-1].reshape(2 * chans, group_rows, chans, group_rows)
    term = jnp.sum(term * jnp.eye(group_rows, dtype=F32)[None, :, None, :], axis=(1, 3))
    own_first = jnp.stack([term[:chans], term[chans:]])
    ordered = jnp.where(core == 0, own_first, own_first[::-1]).reshape(2 * chans, chans)
    ordered = ordered * norm_scale

    pairs(arrived(blocks - 2), [ordered, *tokens])
    spectral_grad = gradient[0]
    lift_own = jnp.sum(sum(sums), axis=(2, 3)).T
    lift_local = jnp.sum(local_sums[-1], axis=(2, 3)).T
    lift_own = jnp.concatenate([lift_own + lift_local[:, :chans], lift_local[:, chans:]], 1) * norm_scale
    packed = all_sum(jnp.concatenate([ordered.reshape(-1), lift_own.reshape(-1)]), ("dp", "blk"))
    local_grad = packed[: ordered.size].reshape(ordered.shape)
    lift_own = packed[ordered.size :].reshape(lift_own.shape)
    theirs = swap_cores(lift_own)
    mine = lift_own[:, :chans] + theirs[:, chans:]
    his = lift_own[:, chans:] + theirs[:, :chans]
    lift_grad = jnp.where(core == 0, jnp.concatenate([mine, his], 1), jnp.concatenate([his, mine], 1))
    return (spectral_grad, local_grad, lift_grad)


def solution(mesh):
    in_specs = (
        P("dp", "parts", "blk", None),
        P("parts", None),
        P("parts", "chan"),
        P("parts", ("blk", "dp"), "chan", None, None),
        P("dp", "chan", "blk", "parts"),
    )
    out_specs = (
        P("parts", ("blk", "dp"), "chan", None, None),
        P("parts", "chan"),
        P("parts", None),
    )
    return jax.shard_map(per_device, mesh=mesh, in_specs=in_specs, out_specs=out_specs, check_vma=False)
```

```python
import functools
import math

import jax
import jax.numpy as jnp
import ml_dtypes
import numpy as np
from jax import lax
from jax.experimental import pallas as pl
from jax.experimental.pallas import tpu as pltpu
from jax.sharding import PartitionSpec as P

BF = jnp.bfloat16
F32 = jnp.float32
TWO_PI = 2.0 * math.pi
CHUNKS = 2
VMEM = 48 * 1024 * 1024


def table(freqs, points, length):
    product = (freqs % length)[:, None] * points[None, :] % length
    angle = np.float32(TWO_PI / length) * product.astype(np.float32)
    return np.cos(angle), np.sin(angle)


def column_table(cells, modes):
    cos, sin = table(np.arange(modes), np.arange(cells), cells)
    return np.ascontiguousarray(np.concatenate([cos, -sin], 0).T).astype(ml_dtypes.bfloat16)


def row_tables(rows, modes, blocks, samples):
    index = np.arange(modes)
    cos, sin = table(np.where(index < modes // 2, index, index - modes), np.arange(rows), rows)
    both = np.stack([cos, sin]).astype(ml_dtypes.bfloat16)
    sub = modes // (blocks * samples)
    piece = sub // CHUNKS
    local = rows // blocks
    out = np.empty((blocks, samples, 2 * modes, local), ml_dtypes.bfloat16)
    for z in range(blocks):
        part = both[:, :, z * local : (z + 1) * local]
        for s in range(samples):
            order = np.concatenate(
                [
                    np.arange(piece) + piece * c + sub * ((s ^ j) + samples * ((z + d) % blocks))
                    for d in range(blocks)
                    for c in range(CHUNKS)
                    for j in range(samples)
                ]
            )
            out[z, s] = part[:, order].reshape(2 * modes, local)
    return out


def gelu_slope(value):
    return 0.5 * (1.0 + lax.erf(value * (1.0 / math.sqrt(2.0)))) + value * jnp.exp(-0.5 * value * value) * (
        1.0 / math.sqrt(2.0 * math.pi)
    )


def lift_rows(fields, lw, chan):
    total = fields[0] * lw[0, chan]
    for j in range(1, len(fields)):
        total = total + fields[j] * lw[j, chan]
    return jnp.tanh(total)


def row_forward(u, row_tab, scale):
    modes, width = row_tab.shape[0] // 2, u.shape[1] // 2
    prod = jnp.dot(row_tab, u, preferred_element_type=F32)
    real = (prod[:modes, :width] + prod[modes:, width:]) * scale
    imag = (prod[:modes, width:] - prod[modes:, :width]) * scale
    return jnp.concatenate([real.astype(BF), imag.astype(BF)], 1)


def split_modes(value, outs, at):
    rows = outs[0][0].shape[1]
    for c, part in enumerate(outs):
        for d, out in enumerate(part):
            lo = (d * len(outs) + c) * rows
            out[at] = value[lo : lo + rows]


def by_part(refs):
    each = len(refs) // CHUNKS
    return [refs[i * each : (i + 1) * each] for i in range(CHUNKS)]


def lift_kernel(bunch, scale, lw, fields, col, row_tab, lifted, *outs):
    group, rows, cells = lifted.shape
    first = pl.program_id(0) * group
    lanes = min(cells, 512)
    for b in range(0, group, bunch):
        for lo in range(0, rows, 16):
            for at in range(0, cells, lanes):
                f = [fields[j, lo : lo + 16, at : at + lanes].astype(F32) for j in range(fields.shape[0])]
                for c in range(b, b + bunch):
                    lifted[c, lo : lo + 16, at : at + lanes] = lift_rows(f, lw, first + c).astype(BF)
        u = jnp.dot(lifted[b : b + bunch].reshape(bunch * rows, cells), col[...], preferred_element_type=F32).astype(BF)
        for c in range(bunch):
            split_modes(row_forward(u[c * rows : (c + 1) * rows], row_tab[...], scale), by_part(outs), b + c)


def slope_kernel(scale, first, lw, fields, col, row_tab, *refs):
    out, token = refs[-2:]
    inputs, rows, cells = fields.shape
    blocks, group, sub = out.shape[0], out.shape[1], out.shape[3]
    for c in range(group):
        chan = first + pl.program_id(0) * group + c
        w = [[] for _ in range(inputs)]
        for lo in range(0, rows, 16):
            f = [fields[j, lo : lo + 16].astype(F32) for j in range(inputs)]
            t = lift_rows(f, lw, chan)
            slope = 1.0 - t * t
            for j in range(inputs):
                w[j].append((f[j] * slope).astype(BF))
        u = jnp.dot(jnp.concatenate(sum(w, []), 0), col[...], preferred_element_type=F32).astype(BF)
        for j in range(inputs):
            v = row_forward(u[j * rows : (j + 1) * rows], row_tab[...], scale)
            for d in range(blocks):
                out[d, c, j] = v[d * sub : (d + 1) * sub]
    token[...] = jnp.zeros(token.shape, F32)


def pair_kernel(n, *refs):
    out, token = refs[-2:]
    for c in range(out.shape[0]):
        back = [b[c].astype(F32) for b in refs[:n]]
        for j in range(out.shape[1]):
            total = None
            for b, f in zip(back, refs[n : 2 * n], strict=True):
                for r in range(0, b.shape[0], 8):
                    prod = b[r : r + 8] * f[0, c, j, r : r + 8].astype(F32)
                    total = prod if total is None else total + prod
            tile = total[:, :128]
            for k in range(128, total.shape[1], 128):
                tile = tile + total[:, k : k + 128]
            out[c, j] = tile
    token[...] = jnp.zeros(token.shape, F32)


def local_kernel(mix, own, other, out, token):
    n, rows, cells = own.shape
    for lo in range(0, cells, 256):
        at = pl.ds(lo, 256)
        both = jnp.concatenate([own[:, :, at].reshape(n * rows, 256), other[:, :, at].reshape(n * rows, 256)], 0)
        got = jnp.dot(mix[...], both, preferred_element_type=F32)
        out[:, :, at] = got.reshape(-1, rows, 256)
    token[...] = jnp.zeros(token.shape, F32)


def local_back_kernel(lw, mix, fields, own, other, grad, *refs):
    earlier, (terms, sums) = refs[:-2], refs[-2:]
    n, rows, cells = own.shape
    inputs = fields.shape[0]

    @pl.when(pl.program_id(0) == 0)
    def _():
        for i, total in enumerate((terms, sums)):
            total[...] = earlier[i][...] if earlier else jnp.zeros(total.shape, F32)

    g = grad[...].reshape(-1, cells)
    for half, part in enumerate((own, other)):
        terms[half] += lax.dot_general(
            part[...].reshape(n * rows, cells), g, (((1,), (1,)), ((), ())), preferred_element_type=F32
        )

    for lo in range(0, cells, 256):
        at = pl.ds(lo, 256)
        back = jnp.dot(mix[...], grad[:, :, at].reshape(-1, 256), preferred_element_type=F32)
        f = [fields[j, :, at].astype(F32) for j in range(inputs)]
        for c in range(2 * n):
            t = lift_rows(f, lw, c)
            total = back[c * rows : (c + 1) * rows] * (1.0 - t * t)
            for j in range(inputs):
                prod = f[j] * total
                prod = prod[:, :128] + prod[:, 128:]
                tile = prod[:8]
                for r in range(8, rows, 8):
                    tile = tile + prod[r : r + 8]
                sums[c, j] += tile


def row_inverse(refs, chan, row_inv):
    rows = row_inv.shape[0] // 2
    width = refs[0].shape[-1] // 2
    hops = (len(refs) - 1) // 2
    blocks = [refs[0][chan]]
    for s in range(hops - 1, -1, -1):
        blocks.append(refs[1 + s][chan] + refs[hops + hops - s][chan])
    prod = jnp.dot(row_inv, jnp.concatenate(blocks, 0), preferred_element_type=F32)
    real = prod[:rows, :width] - prod[rows:, width:]
    imag = prod[:rows, width:] + prod[rows:, :width]
    return jnp.concatenate([real.astype(BF), imag.astype(BF)], 1)


def middle_kernel(blocks, bunch, grid_scale, scale, local, cotan, col, col_inv, row_tab, row_inv, *refs):
    n_in = 2 * blocks - 1
    grad, outs = refs[n_in], refs[n_in + 1 :]
    group, rows, cells = grad.shape
    for b in range(0, group, bunch):
        h = jnp.concatenate([row_inverse(refs[:n_in], c, row_inv[...]) for c in range(b, b + bunch)], 0)
        grid = jnp.dot(h, col_inv[...], preferred_element_type=F32)
        for c in range(bunch):
            for lo in range(0, rows, 16):
                pre = grid[c * rows + lo : c * rows + lo + 16] * grid_scale + local[b + c, lo : lo + 16]
                slope = cotan[0, b + c, lo : lo + 16].astype(F32) * gelu_slope(pre)
                grad[b + c, lo : lo + 16] = slope.astype(BF)
        u = jnp.dot(grad[b : b + bunch].reshape(bunch * rows, cells), col[...], preferred_element_type=F32).astype(BF)
        for c in range(bunch):
            split_modes(row_forward(u[c * rows : (c + 1) * rows], row_tab[...], scale), by_part(outs), b + c)


def mix_kernel(samples, core, w_keep, w_send, *refs):
    xs, keep, send = refs[:samples], refs[samples], refs[samples + 1]
    width = w_keep.shape[-1]
    ins, outs = w_keep.shape[2], w_keep.shape[3]
    for lo in range(0, width, 128):
        re, im = pl.ds(lo, 128), pl.ds(width + lo, 128)
        xr = [x[0, :, re].astype(F32) for x in xs]
        xi = [x[0, :, im].astype(F32) for x in xs]
        for w, out in ((w_keep, keep), (w_send, send)):
            real = [jnp.zeros((outs, 128), F32) for _ in range(samples)]
            imag = [jnp.zeros((outs, 128), F32) for _ in range(samples)]
            for i in range(ins):
                wr = w[0, 0, i, :, re].astype(F32)
                wi = w[1, 0, i, :, re].astype(F32)
                for s in range(samples):
                    a, b = xr[s][i : i + 1], xi[s][i : i + 1]
                    real[s] = real[s] + (wr * a - wi * b)
                    imag[s] = imag[s] + (wr * b + wi * a)
            for s in range(samples):
                out[s, 0, :, re] = real[s].astype(BF)
                out[s, 0, :, im] = imag[s].astype(BF)


def back_kernel(samples, core, w_own, w_other, g_other, *refs):
    gs, out = refs[:samples], refs[samples]
    width = w_own.shape[-1]
    ins, outs = w_own.shape[2], w_own.shape[3]
    for lo in range(0, width, 128):
        re, im = pl.ds(lo, 128), pl.ds(width + lo, 128)
        gr = [[g[0, :, re].astype(F32) for g in gs], [g_other[s, 0, :, re].astype(F32) for s in range(samples)]]
        gi = [[g[0, :, im].astype(F32) for g in gs], [g_other[s, 0, :, im].astype(F32) for s in range(samples)]]
        real = [[] for _ in range(samples)]
        imag = [[] for _ in range(samples)]
        for i in range(ins):
            w = [
                (w_own[0, 0, i, :, re].astype(F32), w_own[1, 0, i, :, re].astype(F32)),
                (w_other[0, 0, i, :, re].astype(F32), w_other[1, 0, i, :, re].astype(F32)),
            ]
            for s in range(samples):
                r = m = None
                for half in range(2):
                    wr, wi = w[half]
                    a, b = gr[half][s], gi[half][s]
                    r1 = wr * a + wi * b
                    m1 = wr * b - wi * a
                    r, m = (r1, m1) if r is None else (r + r1, m + m1)
                real[s].append(jnp.sum(r, axis=0, keepdims=True))
                imag[s].append(jnp.sum(m, axis=0, keepdims=True))
        for s in range(samples):
            out[s, 0, :, re] = jnp.concatenate(real[s], 0).astype(BF)
            out[s, 0, :, im] = jnp.concatenate(imag[s], 0).astype(BF)


def weight_kernel(samples, core, *refs):
    g_other, out, token = refs[0], refs[-2], refs[-1]
    xs, gs = refs[1 : 1 + samples], refs[1 + samples : 1 + 2 * samples]
    ins, half = xs[0].shape[1], gs[0].shape[1]
    width = xs[0].shape[2] // 2
    own = pl.ds(pl.multiple_of(core[0] * half, half), half)
    other = pl.ds(pl.multiple_of((1 - core[0]) * half, half), half)
    for lo in range(0, width, 128):
        re, im = pl.ds(lo, 128), pl.ds(width + lo, 128)
        xr = [x[0, :, re].astype(F32) for x in xs]
        xi = [x[0, :, im].astype(F32) for x in xs]
        for where in (own, other):
            if where is own:
                gr = [g[0, :, re].astype(F32) for g in gs]
                gi = [g[0, :, im].astype(F32) for g in gs]
            else:
                gr = [g_other[s, 0, :, re].astype(F32) for s in range(samples)]
                gi = [g_other[s, 0, :, im].astype(F32) for s in range(samples)]
            for i in range(ins):
                real = imag = None
                for s in range(samples):
                    a, b = xr[s][i : i + 1], xi[s][i : i + 1]
                    r1 = gr[s] * a + gi[s] * b
                    m1 = gi[s] * a - gr[s] * b
                    real, imag = (r1, m1) if real is None else (real + r1, imag + m1)
                out[0, 0, i, where, re] = real.astype(BF)
                out[1, 0, i, where, re] = imag.astype(BF)
    token[...] = jnp.zeros(token.shape, F32)


TOKEN = ((8, 128), F32, (8, 128), lambda i, *_: (0, 0))


def call(body, grid, ins, outs, flops, transcendentals=0, prefetch=None, tokens=(), into=None, vmem=VMEM):
    scalars = 0 if prefetch is None else 1

    def spec(block, index):
        if block is None:
            return pl.BlockSpec(memory_space=pltpu.SMEM)
        return pl.BlockSpec(block, index)

    moved = 0
    for a, block, _ in ins:
        moved += a.size * a.dtype.itemsize if block is None else math.prod(n for n in block if isinstance(n, int)) * math.prod(grid) * a.dtype.itemsize
    moved += sum(math.prod(b) * math.prod(grid) * jnp.dtype(t).itemsize for _, t, b, _ in outs)
    extra = list(tokens) + ([] if into is None else [into])

    def kernel(*refs):
        n = scalars + len(ins)
        body(*refs[:n], *refs[n + len(extra) :])

    return pl.pallas_call(
        kernel,
        grid_spec=pltpu.PrefetchScalarGridSpec(
            num_scalar_prefetch=scalars,
            grid=grid,
            in_specs=[spec(b, i) for _, b, i in ins] + [pl.BlockSpec(memory_space=pl.ANY)] * len(extra),
            out_specs=[spec(b, i) for _, _, b, i in outs],
        ),
        out_shape=[jax.ShapeDtypeStruct(s, t) for s, t, _, _ in outs],
        input_output_aliases={} if into is None else {scalars + len(ins) + len(extra) - 1: 0},
        compiler_params=pltpu.CompilerParams(vmem_limit_bytes=vmem),
        cost_estimate=pl.CostEstimate(flops=int(flops), bytes_accessed=int(moved), transcendentals=int(transcendentals)),
    )(*(() if prefetch is None else (prefetch,)), *[a for a, _, _ in ins], *extra)


def hold(value, *tokens):
    if not tokens:
        return value
    tokens = list(tokens)
    anywhere = pl.BlockSpec(memory_space=pl.ANY)
    return pl.pallas_call(
        lambda *refs: None,
        in_specs=[anywhere] * (1 + len(tokens)),
        out_specs=anywhere,
        out_shape=jax.ShapeDtypeStruct(value.shape, value.dtype),
        input_output_aliases={0: 0},
        cost_estimate=pl.CostEstimate(flops=0, bytes_accessed=0, transcendentals=0),
    )(value, *tokens)


def add_kernel(a, b, c, d, up, down):
    up[...] = (a[...].astype(F32) + b[...].astype(F32)).astype(BF)
    down[...] = (c[...].astype(F32) + d[...].astype(F32)).astype(BF)


def add_pairs(a, b, c, d, tokens):
    n = a.shape[0] // 2
    part = ((n, *a.shape[1:]), lambda i, *_: (i, 0, 0))
    return call(
        add_kernel, (2,), [(v, *part) for v in (a, b, c, d)], [(a.shape, BF, *part)] * 2, 4 * a.size, tokens=tokens
    )


def spaced(fill):
    return [None, *fill]


def run_next(fill, source):
    run = fill.pop(0) if fill else None
    got = [] if run is None else run(source)
    return got if isinstance(got, list) else [got]


def chain_sums(shares, fill):
    hops = len(shares[0]) - 1
    blocks = hops + 1
    got = [None] * len(shares)
    tokens = []
    for t in range(hops):
        for p, part in enumerate(shares):
            up, down = part[hops - t], part[t + 1]
            if t:
                up, down = add_pairs(up, got[p][1], down, got[p][2], tokens)
                tokens = []
            below = lax.ppermute(up, "blk", [(z, z + 1) for z in range(t + 1)])
            above = lax.ppermute(down, "blk", [(blocks - 1 - z, blocks - 2 - z) for z in range(t + 1)])
            got[p] = (part[0], below, above)
            tokens = tokens + run_next(fill, up)
    return got


def chain_gather(own, blocks, below, above, fill):
    tokens = []
    for t in range(blocks - 1):
        if tokens:
            below[-1], above[-1] = hold(below[-1], *tokens), hold(above[-1], *tokens)
        up, down = (below[-1], above[-1]) if t else (own, own)
        below.append(lax.ppermute(up, "blk", [(z, z + 1) for z in range(t, blocks - 1)]))
        above.append(lax.ppermute(down, "blk", [(blocks - 1 - z, blocks - 2 - z) for z in range(t, blocks - 1)]))
        tokens = run_next(fill, up)
    return tokens


def swap_samples(pieces):
    n = len(pieces)
    return [pieces[0]] + [lax.ppermute(pieces[j], "dp", [(i, i ^ j) for i in range(n)]) for j in range(1, n)]


def swap_cores(value):
    return lax.ppermute(value, "chan", [(0, 1), (1, 0)])


def to_modes(parts, samples):
    got = []
    for own, below, above in parts:
        total = (own.astype(F32) + below.astype(F32) + above.astype(F32)).astype(BF).transpose(1, 0, 2)
        sub = total.shape[0] // samples
        got.append((total, swap_samples([total[j * sub : (j + 1) * sub] for j in range(samples)])))
    return got


def from_modes(parts):
    return jnp.concatenate([a for pieces in parts for a in pieces], 0).transpose(1, 0, 2)


def all_sum(value, axes):
    for axis in axes:
        n = lax.axis_size(axis)
        values = [value] + [lax.ppermute(value, axis, [(i, i ^ j) for i in range(n)]) for j in range(1, n)]
        while len(values) > 1:
            values = [a + b for a, b in zip(values[::2], values[1::2], strict=True)]
        value = values[0]
    return value


def per_device(fields, lift_weight, local_weight, spectral_weight, cotangent):
    blocks = lax.axis_size("blk")
    samples = lax.axis_size("dp")
    sample = fields[0]
    inputs, rows, cells = sample.shape
    chans = cotangent.shape[1]
    mode_dev = spectral_weight.shape[1]
    half = spectral_weight.shape[3] // 2
    freqs = spectral_weight.shape[4]
    width = 2 * freqs
    modes = mode_dev * blocks * samples
    sub = modes // blocks
    piece = mode_dev // CHUNKS
    all_rows = rows * blocks
    z, s, core = lax.axis_index("blk"), lax.axis_index("dp"), lax.axis_index("chan")
    core_ref = core.astype(jnp.int32)[None]
    unit_scale = 1.0 / math.sqrt(all_rows * cells)
    norm_scale = 1.0 / math.sqrt(samples * all_rows * cells)

    col = jnp.asarray(column_table(cells, freqs))
    col_inv = jnp.asarray(np.ascontiguousarray(column_table(cells, freqs).T))
    row_all = jnp.asarray(row_tables(all_rows, modes, blocks, samples))
    row_tab = lax.dynamic_slice(row_all, (z, s, 0, 0), (1, 1, 2 * modes, rows))[0, 0]
    row_inv = row_tab.reshape(2, modes, rows).transpose(0, 2, 1).reshape(2 * rows, modes)
    lw_wide = lift_weight.astype(F32)
    own_lw = lax.dynamic_slice_in_dim(lw_wide, core * chans, chans, 1)
    both_lw = jnp.concatenate([own_lw, lax.dynamic_slice_in_dim(lw_wide, (1 - core) * chans, chans, 1)], 1)
    lw_rows = jnp.concatenate(
        [
            lax.dynamic_slice_in_dim(local_weight, core * chans, chans, 0),
            lax.dynamic_slice_in_dim(local_weight, (1 - core) * chans, chans, 0),
        ],
        0,
    )
    group_rows = 16
    eye = jnp.eye(group_rows, dtype=BF)
    spread = (lw_rows[:, None, :, None] * eye[None, :, None, :]).reshape(2 * chans * group_rows, chans * group_rows)

    def whole(a):
        return (a, a.shape, lambda i, *_: (0,) * a.ndim)

    def channel(a, n=1):
        return (a, (n, *a.shape[1:]), lambda i, *_: (i,) + (0,) * (a.ndim - 1))

    def part_outs(n):
        shape = (chans, sub // CHUNKS, width)
        return [(shape, BF, (n, *shape[1:]), lambda i, *_: (i, 0, 0)) for _ in range(CHUNKS * blocks)]

    matrix = chans * rows * 4 * freqs * (cells + 2 * modes)
    group, bunch = math.gcd(chans, 8), math.gcd(chans, 4)
    lifted, *shares = call(
        lambda place, *refs: lift_kernel(bunch, unit_scale, *refs),
        (chans // group,),
        [
            (own_lw, None, None),
            whole(sample),
            whole(col),
            (row_all, (pl.squeezed, pl.squeezed, 2 * modes, rows), lambda i, place: (place[0], place[1], 0, 0)),
        ],
        [((chans, rows, cells), BF, (group, rows, cells), lambda i, *_: (i, 0, 0)), *part_outs(group)],
        matrix,
        chans * rows * cells,
        prefetch=jnp.stack([z, s]).astype(jnp.int32),
    )
    shares = by_part(shares)
    lifted_other = swap_cores(lifted)

    slopes = [None]

    def slope_piece(first, count):
        def run(source):
            got, token = call(
                functools.partial(slope_kernel, unit_scale, first),
                (count // 2,),
                [(own_lw, None, None), whole(sample), whole(col), whole(row_tab)],
                [
                    (
                        (blocks, chans, inputs, sub, width),
                        BF,
                        (blocks, 2, inputs, sub, width),
                        lambda i, *_, first=first: (0, first // 2 + i, 0, 0, 0),
                    ),
                    TOKEN,
                ],
                matrix * inputs * count // chans,
                count * rows * cells,
                tokens=(source,),
                into=slopes[0],
            )
            slopes[0] = got
            return token

        return run

    def together(*runs):
        def run(source):
            return [r(source) for r in runs]

        return run

    locals_ = [None]

    def local_piece(first, count):
        def run(source):
            at = lambda i, *_: (0, first + i, 0)
            locals_[0], token = call(
                local_kernel,
                (count,),
                [
                    whole(spread.T),
                    (lifted, (chans, group_rows, cells), at),
                    (lifted_other, (chans, group_rows, cells), at),
                ],
                [((chans, rows, cells), F32, (chans, group_rows, cells), at), TOKEN],
                4 * chans * chans * group_rows * group_rows * count * cells,
                tokens=(source,),
                into=locals_[0],
            )
            return token

        return run

    def weight_half(part, other):
        return (
            spectral_weight,
            (2, 1, chans, half, freqs),
            lambda i, c, part=part, other=other: (0, part * piece + i, 0, (1 - c[0]) if other else c[0], 0),
        )

    def row_mode(a):
        return (a, (1, *a.shape[1:]), lambda i, *_: (i, 0, 0))

    def stacked(a):
        return (a, (samples, 1, *a.shape[2:]), lambda i, *_: (0, i, 0, 0))

    def stack_out(n):
        return ((samples, piece, n, width), BF, (samples, 1, n, width), lambda i, *_: (0, i, 0, 0))

    mix_flops = 16 * samples * piece * chans * half * freqs
    count = math.gcd(chans, 2)
    slope_fill = [slope_piece(i, count) for i in range(0, chans, count)]
    turns = CHUNKS * (blocks - 1) - 2
    field_modes = []

    arrivals = to_modes(chain_sums(shares, spaced(slope_fill[:turns])), samples)
    parts = []
    for part in range(CHUNKS):
        xs = arrivals[part][1]
        field_modes.append(xs)
        keep, send = call(
            functools.partial(mix_kernel, samples),
            (piece,),
            [weight_half(part, False), weight_half(part, True), *[row_mode(x) for x in xs]],
            [stack_out(half)] * 2,
            mix_flops,
            prefetch=core_ref,
            tokens=[total for total, _ in arrivals[part + 1 :]],
        )
        send = hold(send, *[x for _, later in arrivals[part + 1 :] for x in later[1:]])
        total = (keep.astype(F32) + swap_cores(send).astype(F32)).astype(BF)
        parts.append(swap_samples([total[j] for j in range(samples)]))
    out_modes = from_modes(parts)
    steps = rows // group_rows
    count = -(-steps // 2)
    fill = [local_piece(i, min(count, steps - i)) for i in range(0, steps, count)]
    below, above = [], []
    later = slope_fill[turns:]
    fill[-1] = together(fill[-1], *later[:1])
    fill.append(together(*later[1:3]))
    later = later[3:]
    tokens = chain_gather(out_modes, blocks, below, above, fill)
    while fill:
        tokens = tokens + run_next(fill, out_modes)
    local = locals_[0]

    grad_z, *shares = call(
        functools.partial(middle_kernel, blocks, math.gcd(chans, 2), 2.0 * unit_scale, 2.0 * unit_scale),
        (chans // bunch,),
        [
            channel(local, bunch),
            (cotangent, (1, bunch, rows, cells), lambda i, *_: (0, i, 0, 0)),
            whole(col),
            whole(col_inv),
            whole(row_tab),
            whole(row_inv),
            *[channel(a, bunch) for a in (out_modes, *below, *above)],
        ],
        [((chans, rows, cells), BF, (bunch, rows, cells), lambda i, *_: (i, 0, 0)), *part_outs(bunch)],
        2 * matrix,
        3 * chans * rows * cells,
        tokens=tokens,
        vmem=60 * 1024 * 1024,
    )
    shares = by_part(shares)

    terms, local_sums = [], []

    def back_piece(first, count):
        at = lambda i, *_: (0, first + i, 0)

        def run(source):
            t, v = call(
                local_back_kernel,
                (count,),
                [
                    (both_lw, None, None),
                    whole(spread),
                    (sample, (inputs, group_rows, cells), at),
                    (lifted, (chans, group_rows, cells), at),
                    (lifted_other, (chans, group_rows, cells), at),
                    (grad_z, (chans, group_rows, cells), at),
                    *[whole(a) for a in (*terms[-1:], *local_sums[-1:])],
                ],
                [
                    (
                        (2, chans * group_rows, chans * group_rows),
                        F32,
                        (2, chans * group_rows, chans * group_rows),
                        lambda i, *_: (0, 0, 0),
                    ),
                    ((2 * chans, inputs, 8, 128), F32, (2 * chans, inputs, 8, 128), lambda i, *_: (0, 0, 0, 0)),
                ],
                8 * chans * chans * group_rows * group_rows * count * cells,
                2 * chans * group_rows * count * cells,
                tokens=(source,),
            )
            terms.append(t)
            local_sums.append(v)
            return v

        return run

    steps = rows // group_rows
    count = -(-steps // 8)
    back_fill = [back_piece(i, min(count, steps - i)) for i in range(0, steps, count)]
    grad_modes, grad_others = [], []

    arrivals = to_modes(chain_sums(shares, spaced([together(*back_fill[:3]), *back_fill[3 : turns + 2]])), samples)
    parts = []
    for part in range(CHUNKS):
        gs = arrivals[part][1]
        other = swap_cores(jnp.stack(gs))
        grad_modes.append(gs)
        grad_others.append(other)
        (back,) = call(
            functools.partial(back_kernel, samples),
            (piece,),
            [weight_half(part, False), weight_half(part, True), stacked(other), *[row_mode(g) for g in gs]],
            [stack_out(chans)],
            mix_flops,
            prefetch=core_ref,
            tokens=[total for total, _ in arrivals[part + 1 :]],
        )
        parts.append(swap_samples([back[j] for j in range(samples)]))
    back_modes = from_modes(parts)
    below, above = [], []

    gradient = [None]

    def weight_piece(part):
        def run(source):
            gradient[0], token = call(
                functools.partial(weight_kernel, samples),
                (piece,),
                [
                    stacked(grad_others[part]),
                    *[row_mode(x) for x in field_modes[part]],
                    *[row_mode(g) for g in grad_modes[part]],
                ],
                [
                    (
                        (2, mode_dev, chans, 2 * half, freqs),
                        BF,
                        (2, 1, chans, 2 * half, freqs),
                        lambda i, *_: (0, part * piece + i, 0, 0, 0),
                    ),
                    TOKEN,
                ],
                mix_flops,
                prefetch=core_ref,
                tokens=(source,),
                into=gradient[0],
            )
            return token

        return run

    sums = []
    at_once = 4

    def pairs(modes_of, tokens=()):
        def spectra(d):
            return (slopes[0], (1, at_once, inputs, sub, width), lambda i, *_: (d, i, 0, 0, 0))

        got, token = call(
            functools.partial(pair_kernel, len(modes_of)),
            (chans // at_once,),
            [channel(a, at_once) for _, a in modes_of] + [spectra(d) for d, _ in modes_of],
            [((chans, inputs, 8, 128), F32, (at_once, inputs, 8, 128), lambda i, *_: (i, 0, 0, 0)), TOKEN],
            4 * len(modes_of) * chans * inputs * sub * width,
            tokens=tokens,
        )
        sums.append(got)
        return token

    def arrived(t):
        return [(blocks - 1 - t, below[t]), (1 + t, above[t])]

    def pair_piece(t):
        return lambda source: pairs(([(0, back_modes)] if t == 0 else []) + arrived(t), [source])

    fill = [
        together(*[weight_piece(part) for part in range(CHUNKS)]),
        together(*back_fill[turns + 2 :], *later),
        together(*[pair_piece(t) for t in range(min(2, blocks - 2))]),
    ]
    fill += [pair_piece(t) for t in range(2, blocks - 2)]
    tokens = chain_gather(back_modes, blocks, below, above, fill)
    while fill:
        tokens = tokens + run_next(fill, back_modes)
    term = terms[-1].reshape(2 * chans, group_rows, chans, group_rows)
    term = jnp.sum(term * jnp.eye(group_rows, dtype=F32)[None, :, None, :], axis=(1, 3))
    own_first = jnp.stack([term[:chans], term[chans:]])
    ordered = jnp.where(core == 0, own_first, own_first[::-1]).reshape(2 * chans, chans)
    ordered = ordered * norm_scale

    pairs(arrived(blocks - 2), [ordered, *tokens])
    spectral_grad = gradient[0]
    lift_own = jnp.sum(sum(sums), axis=(2, 3)).T
    lift_local = jnp.sum(local_sums[-1], axis=(2, 3)).T
    lift_own = jnp.concatenate([lift_own + lift_local[:, :chans], lift_local[:, chans:]], 1) * norm_scale
    packed = all_sum(jnp.concatenate([ordered.reshape(-1), lift_own.reshape(-1)]), ("dp", "blk"))
    local_grad = packed[: ordered.size].reshape(ordered.shape)
    lift_own = packed[ordered.size :].reshape(lift_own.shape)
    theirs = swap_cores(lift_own)
    mine = lift_own[:, :chans] + theirs[:, chans:]
    his = lift_own[:, chans:] + theirs[:, :chans]
    lift_grad = jnp.where(core == 0, jnp.concatenate([mine, his], 1), jnp.concatenate([his, mine], 1))
    return (spectral_grad, local_grad, lift_grad)


def solution(mesh):
    in_specs = (
        P("dp", "parts", "blk", None),
        P("parts", None),
        P("parts", "chan"),
        P("parts", ("blk", "dp"), "chan", None, None),
        P("dp", "chan", "blk", "parts"),
    )
    out_specs = (
        P("parts", ("blk", "dp"), "chan", None, None),
        P("parts", "chan"),
        P("parts", None),
    )
    return jax.shard_map(per_device, mesh=mesh, in_specs=in_specs, out_specs=out_specs, check_vma=False)
```
